32 devices in a mesh: batch: 8 (over z, core), head: 4 (over y, x).
Axes of the slice: x: 2, y: 2, z: 4, core: 2. Of those that a mesh axis runs over, the one named last changes fastest.
Arguments:
- tokens: bfloat16 [8192, 2048], P(('batch', 'head')), may hold values from -6 to 6
- attention_gain: float32 [2048], replicated, may hold values from 0.25 to 1.75
- query_down: bfloat16 [2048, 1024], replicated, may hold values from -0.125 to 0.125
- query_gain: float32 [1024], replicated, may hold values from 0.25 to 1.75
- query_up: bfloat16 [1024, 4096], P(None, 'head'), may hold values from -0.1875 to 0.1875
- key_weight: bfloat16 [2048, 256], replicated, may hold values from -0.25 to 0.25
- value_weight: bfloat16 [2048, 256], replicated, may hold values from -0.125 to 0.125
- out_weight: bfloat16 [4096, 2048], P('head'), may hold values from -0.375 to 0.375
- feed_gain: float32 [2048], replicated, may hold values from 0.25 to 1.75
- gate_weight: bfloat16 [2048, 5632], P(('batch', 'head')), may hold values from -0.125 to 0.125
- up_weight: bfloat16 [2048, 5632], P(('batch', 'head')), may hold values from -0.125 to 0.125
- down_weight: bfloat16 [5632, 2048], P(None, ('batch', 'head')), may hold values from -0.078125 to 0.078125
- lengths: int32 [8, 3], P('batch'), may hold values from 0 to 1024, as said below
- cotangent: bfloat16 [8192, 2048], P(('batch', 'head')), may hold values from -6 to 6
Outputs:
- output: bfloat16 [8192, 2048], P(('batch', 'head'))
- input_gradient: float32 [8192, 2048], P(('batch', 'head'))
- attention_gain_gradient: float32 [2048], replicated
- query_down_gradient: float32 [2048, 1024], replicated
- query_gain_gradient: float32 [1024], replicated
- query_up_gradient: float32 [1024, 4096], P(None, 'head')
- key_weight_gradient: float32 [2048, 256], replicated
- value_weight_gradient: float32 [2048, 256], replicated
- out_weight_gradient: float32 [4096, 2048], P('head')
- feed_gain_gradient: float32 [2048], replicated
- gate_weight_gradient: float32 [2048, 5632], P(('batch', 'head'))
- up_weight_gradient: float32 [2048, 5632], P(('batch', 'head'))
- down_weight_gradient: float32 [5632, 2048], P(None, ('batch', 'head'))
The draws below stay inside these ranges and needn't reach their ends.
Inputs may be any that keep to these rules, and one draw needn't show every extreme that they name: In each batch group's row the first and the last length lie from 0 to 255 and the three lengths sum to 1024; batch group 0 is one whole document.
All inputs are finite; a program needn't handle non-finite values.
Results may differ from the reference program's by a relative error of at most 0.02.
Values may be sent and summed in bfloat16 or wider, within the bound.
No kernel may reach another device: no remote copies, remote signals or barrier semaphores. Data moves between devices by JAX's collectives and lax.ppermute only.
A program may use at most 576 MiB of HBM per device.

```python
import math
import jax
import jax.numpy as jnp
from jax import lax

D = 2048
QR = 1024
QH = 16
HD = 256
FF = 5632
GROUP_TOK = 1024
BLOCK = 512
ROWS = 256
TOKENS = 8192
N_BATCH = 8


def draw_lengths(key, part):
    key = jax.random.fold_in(key, 7)
    ends = jax.random.randint(key, (N_BATCH, 2), 0, ROWS, dtype=jnp.int32)
    keep = (jnp.arange(N_BATCH, dtype=jnp.int32) != 0).astype(jnp.int32)[:, None]
    ends = ends * keep
    middle = GROUP_TOK - ends[:, 0] - ends[:, 1]
    return jnp.stack([ends[:, 0], middle, ends[:, 1]], axis=1).astype(jnp.int32)


def with_spikes(drawn, own_key, source, target, blocks, factor):
    def block_of(dim):
        return (jnp.arange(drawn.shape[dim]) // (drawn.shape[dim] // blocks)).reshape((-1,) + (1,) * (drawn.ndim - 1 - dim))

    near = jax.random.permutation(own_key, blocks)[block_of(target)]
    other_side = (block_of(target) + blocks // 2) % blocks
    return jnp.where((block_of(source) == near) | (block_of(source) == other_side), factor * drawn, drawn)


def level_of(stream_key, dims, split, low, high):
    def one(axis_at, shards_of):
        steps = jax.random.uniform(jax.random.fold_in(jax.random.fold_in(stream_key, 6), axis_at), (shards_of,), jnp.float32, low / len(split), high / len(split))
        return jnp.repeat(jnp.exp(steps), dims[axis_at] // shards_of).reshape((-1,) + (1,) * (len(dims) - axis_at - 1))

    level = one(*split[0])
    for cut in split[1:]:
        level = level * one(*cut)
    return level


def centred(stream_key, shape, deviation, limit, split=(), held_as=jnp.bfloat16):
    level = level_of(stream_key, shape, split, -0.22, 0.18) if split else 1.0
    entries = jax.random.normal(stream_key, shape, jnp.float32) * deviation * level
    return jnp.minimum(jnp.maximum(entries, -limit), limit).astype(held_as)


def bell_draw_with(key, dims, spread, limit, pieces, heavy, kind=jnp.bfloat16):
    entries = spread * jax.random.normal(key, dims, jnp.float32)
    if pieces:
        entries = entries * level_of(key, dims, pieces, -0.22, 0.18)
    return jnp.clip(with_spikes(entries, jax.random.fold_in(key, 3), *heavy), -limit, limit).astype(kind)


def setup_inputs(seed: int = 0) -> dict:
    seeds = jax.random.split(jax.random.key(seed), 15)
    tokens = centred(seeds[0], (TOKENS, D), 1.0, 6.0, ((0, 32),))
    attention_gain = jnp.clip(1.0 + 0.15 * jax.random.normal(seeds[1], (D,), jnp.float32), 0.25, 1.75)
    query_down = centred(seeds[2], (D, QR), D ** -0.5, 0.125)
    query_gain = jnp.clip(1.0 + 0.15 * jax.random.normal(seeds[3], (QR,), jnp.float32), 0.25, 1.75)
    query_up = centred(seeds[4], (QR, QH * HD), QR ** -0.5, 0.1875, ((1, 4),))
    key_weight = centred(seeds[5], (D, HD), (D // 4) ** -0.5, 0.25)
    value_weight = centred(seeds[6], (D, HD), D ** -0.5, 0.125)
    out_weight = centred(seeds[7], (QH * HD, D), (QH * HD // 16) ** -0.5, 0.375, ((0, 4),))
    feed_gain = jnp.clip(1.0 + 0.15 * jax.random.normal(seeds[8], (D,), jnp.float32), 0.25, 1.75)
    gate_weight = centred(seeds[9], (D, FF), D ** -0.5, 0.125, ((0, 32),))
    up_weight = centred(seeds[10], (D, FF), D ** -0.5, 0.125, ((0, 32),))
    down_weight = centred(seeds[11], (FF, D), FF ** -0.5, 0.078125, ((1, 32),))
    lengths = draw_lengths(jax.random.fold_in(seeds[14], 71), 0)
    cotangent = bell_draw_with(seeds[13], (TOKENS, D), 1.0, 6.0, ((0, 32),), (0, 1, 32, 2.75))
    return {"tokens": tokens, "attention_gain": attention_gain, "query_down": query_down, "query_gain": query_gain, "query_up": query_up, "key_weight": key_weight, "value_weight": value_weight, "out_weight": out_weight, "feed_gain": feed_gain, "gate_weight": gate_weight, "up_weight": up_weight, "down_weight": down_weight, "lengths": lengths, "cotangent": cotangent}


@jax.custom_vjp
def low(v):
    return lax.optimization_barrier(v.astype(jnp.bfloat16)).astype(jnp.float32)

@jax.custom_vjp
def low_back(v):
    return v

def low_keep(v):
    return (low(v), None)

def low_pass(kept, grad):
    return (grad,)

def back_keep(v):
    return (v, None)

def back_low(kept, grad):
    return (low(grad),)
low.defvjp(low_keep, low_pass)
low_back.defvjp(back_keep, back_low)
epsilon = 1e-05
masked_value = -1e+30

def product(left, right):
    return jnp.dot(left, right, precision=lax.Precision.HIGHEST, preferred_element_type=jnp.float32)

def rescale(values, gain):
    return values * lax.rsqrt(lax.optimization_barrier(jnp.mean(values * values, axis=-1, keepdims=True)) + epsilon) * gain

def document_places(counts, total):
    bounds = jnp.cumsum(counts.reshape(-1), dtype=jnp.int32)
    index = jnp.arange(total, dtype=jnp.int32)
    segment = (index >= bounds[0]).astype(jnp.int32) + (index >= bounds[1]).astype(jnp.int32)
    begin = jnp.where(segment == 0, 0, jnp.where(segment == 1, bounds[0], bounds[1])).astype(jnp.int32)
    return (segment, index - begin)

def rotary_tables(place, width):
    half = width // 2
    rates = 10000.0 ** (-2.0 * jnp.arange(half, dtype=jnp.float32) / width)
    turns = place.astype(jnp.float32)[:, None] * rates[None, :]
    return (jnp.cos(turns), jnp.sin(turns))

def rotate(values, cosine, sine):
    half = values.shape[-1] // 2
    first = values[..., :half]
    second = values[..., half:]
    return jnp.concatenate([first * cosine - second * sine, second * cosine + first * sine], axis=-1)

def attend(query, keys, values, segment):
    count_blocks = GROUP_TOK // BLOCK
    scale_factor = 1.0 / math.sqrt(HD)
    key_index = jnp.arange(GROUP_TOK, dtype=jnp.int32)

    @jax.checkpoint
    def one_block(item):
        query_block, segment_block, begin = item
        query_index = begin + jnp.arange(BLOCK, dtype=jnp.int32)
        scores = low_back(jnp.einsum('qhd,kd->hqk', query_block, keys, precision=lax.Precision.HIGHEST) * scale_factor)
        allowed = (segment_block[:, None] == segment[None, :]) & (key_index[None, :] <= query_index[:, None])
        scores = jnp.where(allowed[None], scores, masked_value)
        top = lax.optimization_barrier(jnp.max(scores, axis=-1, keepdims=True))
        raised = jnp.exp(scores - top)
        shares = raised / lax.optimization_barrier(jnp.sum(raised, axis=-1, keepdims=True))
        return jnp.einsum('hqk,kd->qhd', low(shares), values, precision=lax.Precision.HIGHEST)
    starts = jnp.arange(count_blocks, dtype=jnp.int32) * BLOCK
    mixed = lax.map(one_block, (query.reshape(count_blocks, BLOCK, QH, HD), segment.reshape(count_blocks, BLOCK), starts))
    return mixed.reshape(GROUP_TOK, QH * HD)

def layer(inputs, params, segment, place):
    attention_gain, query_down, query_gain, query_up, key_weight, value_weight, out_weight, feed_gain, gate_weight, up_weight, down_weight = params
    cosine, sine = rotary_tables(place, HD)
    normed = low(rescale(inputs, attention_gain))
    latent = low_back(product(normed, query_down))
    latent_in = low(rescale(latent, query_gain))
    query_raw = low_back(product(latent_in, query_up)).reshape(GROUP_TOK, QH, HD)
    query = low(rotate(query_raw, cosine[:, None, :], sine[:, None, :]))
    keys = low(rotate(low_back(product(normed, key_weight)), cosine, sine))
    values = low(low_back(product(normed, value_weight)))
    mixed = low(low_back(attend(query, keys, values, segment)))
    middle = inputs + low_back(product(mixed, out_weight))
    inner = low(rescale(middle, feed_gain))
    gate = low_back(product(inner, gate_weight))
    up = low_back(product(inner, up_weight))
    hidden = low(jax.nn.silu(gate) * up)
    return middle + product(hidden, down_weight)

def reference(tokens, attention_gain, query_down, query_gain, query_up, key_weight, value_weight, out_weight, feed_gain, gate_weight, up_weight, down_weight, lengths, cotangent):
    weights = tuple((item.astype(jnp.float32) for item in (attention_gain, query_down, query_gain, query_up, key_weight, value_weight, out_weight, feed_gain, gate_weight, up_weight, down_weight)))
    grouped = tokens.astype(jnp.float32).reshape(N_BATCH, GROUP_TOK, D)
    grouped_cot = cotangent.astype(jnp.float32).reshape(N_BATCH, GROUP_TOK, D)

    def group_step(totals, item):
        block_in, block_cot, counts = item
        segment, place = document_places(counts, GROUP_TOK)

        def forward(values, *params):
            return layer(values, params, segment, place)
        result, pullback = jax.vjp(forward, block_in, *weights)
        grads = pullback(block_cot)
        totals = tuple((left + right for left, right in zip(totals, grads[1:])))
        return (totals, (result.astype(jnp.bfloat16), grads[0]))
    zeros = tuple((jnp.zeros(item.shape, jnp.float32) for item in weights))
    totals, (outputs, input_grads) = lax.scan(group_step, zeros, (grouped, grouped_cot, lengths))
    return (outputs.reshape(TOKENS, D), input_grads.reshape(TOKENS, D), totals[0], totals[1], totals[2], totals[3], totals[4], totals[5], totals[6], totals[7], totals[8], totals[9], totals[10])
```

```python
import math

import jax
import jax.numpy as jnp
from jax import lax
from jax.sharding import PartitionSpec as P

epsilon = 1e-05
masked_value = -1e30
low = jnp.bfloat16


def dot(left, right, contract=(1, 0)):
    return lax.dot_general(
        left,
        right,
        (((contract[0],), (contract[1],)), ((), ())),
        preferred_element_type=jnp.float32,
    )


def rescale(values, gain):
    factor = lax.rsqrt(jnp.mean(values * values, axis=-1, keepdims=True) + epsilon)
    return (values * factor * gain, factor)


def rescale_back(values, factor, gain, upstream):
    weighted = upstream * gain
    inner_mean = jnp.mean(values * weighted, axis=-1, keepdims=True)
    back = factor * weighted - values * (factor * factor * factor) * inner_mean
    return (back, jnp.sum(upstream * values * factor, axis=0))


def rotate(values, cosine, sine):
    half = values.shape[-1] // 2
    first = values[..., :half]
    second = values[..., half:]
    return jnp.concatenate(
        [first * cosine - second * sine, second * cosine + first * sine], axis=-1
    )


def rotate_back(grads, cosine, sine):
    return rotate(grads, cosine, -sine)


def swap(values, axis, bit):
    size = lax.axis_size(axis)
    return lax.ppermute(values, axis, [(i, i ^ bit) for i in range(size)])


def gather_near(own):
    size = lax.axis_size("head")
    if size == 4:
        cut = own.shape[0] // 2
        first, second = swap(own, "head", 1), swap(own, "head", 2)
        third = jnp.concatenate(
            [swap(first[:cut], "head", 2), swap(second[cut:], "head", 1)], axis=0
        )
        return [own, first, second, third]
    blocks = [own]
    bit = 1
    while bit < size:
        blocks = blocks + [swap(block, "head", bit) for block in blocks]
        bit *= 2
    return blocks


def scatter_near(parts):
    size = len(parts)
    if size == 4:
        cut = parts[0].shape[0] // 2
        via_first = swap(parts[3][:cut], "head", 1)
        via_second = swap(parts[3][cut:], "head", 2)
        second = jnp.concatenate([parts[2][:cut] + via_first, parts[2][cut:]], axis=0)
        first = jnp.concatenate([parts[1][:cut], parts[1][cut:] + via_second], axis=0)
        return (
            parts[0].astype(jnp.float32)
            + swap(first, "head", 1).astype(jnp.float32)
            + swap(second, "head", 2).astype(jnp.float32)
        )
    bit = size // 2
    while bit:
        parts = [parts[k] + swap(parts[k + bit], "head", bit) for k in range(bit)]
        bit //= 2
    return parts[0].astype(jnp.float32)


def spread(pieces):
    return [pieces[0]] + [swap(pieces[k], "head", k) for k in range(1, len(pieces))]


def shards(
    tokens,
    attention_gain,
    query_down,
    query_gain,
    query_up,
    key_weight,
    value_weight,
    out_weight,
    feed_gain,
    gate_weight,
    up_weight,
    down_weight,
    lengths,
    cotangent,
):
    rows, width = tokens.shape
    count = lax.axis_size("head")
    me = lax.axis_index("head")
    total = rows * count
    head_width = key_weight.shape[1]
    local_heads = query_up.shape[1] // head_width
    rank = query_up.shape[0]
    scale_factor = 1.0 / math.sqrt(head_width)
    feed = gate_weight.shape[1]
    feed_part = feed // count
    strip = gate_weight.shape[0]

    stacked = jnp.stack([gate_weight, up_weight, down_weight.T])
    pieces = [
        lax.dynamic_slice_in_dim(stacked, (me ^ k) * feed_part, feed_part, 2) for k in range(count)
    ]
    arrived = spread(pieces)
    columns = jnp.zeros((3, strip * count, feed_part), low)
    for k in range(count):
        columns = lax.dynamic_update_slice(columns, arrived[k], (0, (me ^ k) * strip, 0))
    gate_whole, up_whole, down_whole = (
        lax.all_gather(columns[i], "batch", axis=0, tiled=True) for i in range(3)
    )

    bounds = jnp.cumsum(lengths.reshape(-1), dtype=jnp.int32)
    index = jnp.concatenate(
        [(me ^ k) * rows + jnp.arange(rows, dtype=jnp.int32) for k in range(count)]
    )
    segment = (index >= bounds[0]).astype(jnp.int32) + (index >= bounds[1]).astype(jnp.int32)
    begin = jnp.where(segment == 0, 0, jnp.where(segment == 1, bounds[0], bounds[1]))
    half = head_width // 2
    rates = 10000.0 ** (-2.0 * jnp.arange(half, dtype=jnp.float32) / head_width)
    turns = (index - begin).astype(jnp.float32)[:, None] * rates[None, :]
    cosine, sine = jnp.cos(turns), jnp.sin(turns)
    own_cosine, own_sine = cosine[:rows], sine[:rows]
    allowed = (segment[:, None] == segment[None, :]) & (index[None, :] <= index[:, None])

    inputs = tokens.astype(jnp.float32)
    normed, first_factor = rescale(inputs, attention_gain)
    normed_low = normed.astype(low)
    latent = dot(normed_low, query_down)
    latent_in, latent_factor = rescale(latent, query_gain)
    key_own = rotate(dot(normed_low, key_weight), own_cosine, own_sine).astype(low)
    value_own = dot(normed_low, value_weight).astype(low)
    lkv = jnp.concatenate(
        gather_near(jnp.concatenate([latent_in.astype(low), key_own, value_own], axis=1)), axis=0
    )
    latent_all = lkv[:, :rank]
    keys_all = lkv[:, rank : rank + head_width]
    values_all = lkv[:, rank + head_width :]

    query_raw = dot(latent_all, query_up).reshape(total, local_heads, head_width)
    query_low = rotate(query_raw, cosine[:, None, :], sine[:, None, :]).astype(low)
    scores = (
        jnp.einsum("qhd,kd->hqk", query_low, keys_all, preferred_element_type=jnp.float32)
        * scale_factor
    )
    scores = jnp.where(allowed[None], scores, masked_value)
    top = jnp.max(scores, axis=-1, keepdims=True)
    raised = jnp.exp(scores - top)
    summed = jnp.sum(raised, axis=-1, keepdims=True)
    shares = raised / summed
    shares_low = shares.astype(low)
    mixed_low = (
        jnp.einsum("hqk,kd->qhd", shares_low, values_all, preferred_element_type=jnp.float32)
        .astype(low)
        .reshape(total, local_heads * head_width)
    )
    attention_partial = dot(mixed_low, out_weight).astype(low)
    attention_part = scatter_near(
        [attention_partial[k * rows : (k + 1) * rows] for k in range(count)]
    )
    middle = inputs + attention_part
    inner, second_factor = rescale(middle, feed_gain)
    inner_all = jnp.concatenate(gather_near(inner.astype(low)), axis=0)
    cotangent_all = jnp.concatenate(gather_near(cotangent), axis=0)
    gate = dot(inner_all, gate_whole)
    up = dot(inner_all, up_whole)
    sigma = jax.nn.sigmoid(gate)
    swish = gate * sigma
    hidden_low = (swish * up).astype(low)
    feed_partial = dot(hidden_low, down_whole, (1, 1)).astype(low)
    feed_out = scatter_near([feed_partial[k * rows : (k + 1) * rows] for k in range(count)])
    output = (middle + feed_out).astype(low)

    grad_hidden = dot(cotangent_all, down_whole)
    slope = sigma * (1.0 + gate * (1.0 - sigma))
    grad_gate_low = (grad_hidden * up * slope).astype(low)
    grad_up_low = (grad_hidden * swish).astype(low)
    grad_inner_partial = (
        dot(grad_gate_low, gate_whole, (1, 1)) + dot(grad_up_low, up_whole, (1, 1))
    ).astype(low)
    grad_inner = scatter_near(
        [grad_inner_partial[k * rows : (k + 1) * rows] for k in range(count)]
    )
    sums = [
        lax.psum_scatter(dot(a, b, (0, 0)).astype(low), "batch", scatter_dimension=0, tiled=True)
        for a, b in (
            (cotangent_all, hidden_low),
            (inner_all, grad_gate_low),
            (inner_all, grad_up_low),
        )
    ]
    summed_weights = jnp.stack([sums[1], sums[2], sums[0]])
    pieces = [
        lax.dynamic_slice_in_dim(summed_weights, (me ^ k) * strip, strip, 1) for k in range(count)
    ]
    arrived = spread(pieces)
    feed_gradients = jnp.zeros((3, strip, feed), jnp.float32)
    for k in range(count):
        feed_gradients = lax.dynamic_update_slice(
            feed_gradients, arrived[k].astype(jnp.float32), (0, 0, (me ^ k) * feed_part)
        )

    middle_part, feed_gain_part = rescale_back(middle, second_factor, feed_gain, grad_inner)
    grad_middle = cotangent.astype(jnp.float32) + middle_part
    branch_all = jnp.concatenate(gather_near(grad_middle.astype(low)), axis=0)
    out_gradient = lax.psum(dot(mixed_low, branch_all, (0, 0)).astype(low), "batch")
    grad_mixed_low = dot(branch_all, out_weight, (1, 1)).astype(low).reshape(
        total, local_heads, head_width
    )
    grad_shares = jnp.einsum(
        "qhd,kd->hqk", grad_mixed_low, values_all, preferred_element_type=jnp.float32
    )
    centre = jnp.sum(shares * grad_shares, axis=-1, keepdims=True)
    grad_scores_low = (shares * (grad_shares - centre)).astype(low)
    query_grad = (
        jnp.einsum("hqk,kd->qhd", grad_scores_low, keys_all, preferred_element_type=jnp.float32)
        * scale_factor
    )
    key_grads = (
        jnp.einsum("hqk,qhd->kd", grad_scores_low, query_low, preferred_element_type=jnp.float32)
        * scale_factor
    )
    value_grads = jnp.einsum(
        "hqk,qhd->kd", shares_low, grad_mixed_low, preferred_element_type=jnp.float32
    )
    query_grad_low = (
        rotate_back(query_grad, cosine[:, None, :], sine[:, None, :])
        .astype(low)
        .reshape(total, local_heads * head_width)
    )
    latent_partial = dot(query_grad_low, query_up, (1, 1))
    lkv_partial = jnp.concatenate([latent_partial, key_grads, value_grads], axis=1).astype(low)
    query_up_gradient = lax.psum(dot(latent_all, query_grad_low, (0, 0)).astype(low), "batch")
    lkv_back = scatter_near([lkv_partial[k * rows : (k + 1) * rows] for k in range(count)])
    latent_grad, query_gain_part = rescale_back(
        latent, latent_factor, query_gain, lkv_back[:, :rank]
    )
    key_back = rotate_back(lkv_back[:, rank : rank + head_width], own_cosine, own_sine)
    lkv_grad_low = jnp.concatenate(
        [latent_grad, key_back, lkv_back[:, rank + head_width :]], axis=1
    ).astype(low)

    slice_width = width // count
    normed_slices = jnp.concatenate(
        spread(
            [
                lax.dynamic_slice_in_dim(normed_low, (me ^ k) * slice_width, slice_width, 1)
                for k in range(count)
            ]
        ),
        axis=0,
    )
    lkv_grad_all = jnp.concatenate(gather_near(lkv_grad_low), axis=0)
    shared_part = dot(normed_slices, lkv_grad_all, (0, 0)).astype(low)
    shared_sum = lax.psum(shared_part, "batch")
    shared_all = lax.all_gather(shared_sum, "head", axis=0, tiled=True).astype(jnp.float32)

    grad_normed = (
        dot(lkv_grad_low[:, :rank], query_down, (1, 1))
        + dot(lkv_grad_low[:, rank : rank + head_width], key_weight, (1, 1))
        + dot(lkv_grad_low[:, rank + head_width :], value_weight, (1, 1))
    )
    input_part, attention_gain_part = rescale_back(
        inputs, first_factor, attention_gain, grad_normed
    )
    input_gradient = grad_middle + input_part
    gains = lax.psum(
        jnp.concatenate([attention_gain_part, feed_gain_part, query_gain_part]), ("batch", "head")
    )
    return (
        output,
        input_gradient,
        gains[:width],
        shared_all[:, :rank],
        gains[2 * width :],
        query_up_gradient.astype(jnp.float32),
        shared_all[:, rank : rank + head_width],
        shared_all[:, rank + head_width :],
        out_gradient.astype(jnp.float32),
        gains[width : 2 * width],
        feed_gradients[0],
        feed_gradients[1],
        feed_gradients[2].T,
    )


def solution(mesh):
    rows = P(("batch", "head"), None)
    columns = P(None, ("batch", "head"))
    return jax.shard_map(
        shards,
        mesh=mesh,
        in_specs=(
            rows,
            P(),
            P(),
            P(),
            P(None, "head"),
            P(),
            P(),
            P("head", None),
            P(),
            rows,
            rows,
            columns,
            P("batch", None),
            rows,
        ),
        out_specs=(
            rows,
            rows,
            P(),
            P(),
            P(),
            P(None, "head"),
            P(),
            P(),
            P("head", None),
            P(),
            rows,
            rows,
            columns,
        ),
        check_vma=False,
    )
```

```python
import functools
import math

import jax
import jax.numpy as jnp
from jax import lax
from jax.experimental import pallas as pl
from jax.experimental.pallas import tpu as pltpu
from jax.sharding import PartitionSpec as P

epsilon = 1e-05
masked_value = -1e30
low = jnp.bfloat16


def dot(left, right, contract=(1, 0)):
    return lax.dot_general(
        left,
        right,
        (((contract[0],), (contract[1],)), ((), ())),
        preferred_element_type=jnp.float32,
    )


def rescale(values, gain):
    factor = lax.rsqrt(jnp.mean(values * values, axis=-1, keepdims=True) + epsilon)
    return (values * factor * gain, factor)


def rescale_back(values, factor, gain, upstream):
    weighted = upstream * gain
    inner_mean = jnp.mean(values * weighted, axis=-1, keepdims=True)
    back = factor * weighted - values * (factor * factor * factor) * inner_mean
    return (back, jnp.sum(upstream * values * factor, axis=0))


def rotate(values, cosine, sine):
    half = values.shape[-1] // 2
    first = values[..., :half]
    second = values[..., half:]
    return jnp.concatenate(
        [first * cosine - second * sine, second * cosine + first * sine], axis=-1
    )


def rotate_back(grads, cosine, sine):
    return rotate(grads, cosine, -sine)


def swap(values, axis, bit):
    size = lax.axis_size(axis)
    return lax.ppermute(values, axis, [(i, i ^ bit) for i in range(size)])


def sending_order(size):
    if size == 4:
        return [[3], [1, 2], [0]]
    return [list(range(size))]


def gather_near(own):
    size = lax.axis_size("head")
    if size == 4:
        cut = own.shape[0] // 2
        first, second = swap(own, "head", 1), swap(own, "head", 2)
        third = jnp.concatenate(
            [swap(first[:cut], "head", 2), swap(second[cut:], "head", 1)], axis=0
        )
        return [own, first, second, third]
    blocks = [own]
    bit = 1
    while bit < size:
        blocks = blocks + [swap(block, "head", bit) for block in blocks]
        bit *= 2
    return blocks


def scatter_near(parts):
    size = len(parts)
    if size == 4:
        cut = parts[0].shape[0] // 2
        via_first = swap(parts[3][:cut], "head", 1)
        via_second = swap(parts[3][cut:], "head", 2)
        second = jnp.concatenate([parts[2][:cut] + via_first, parts[2][cut:]], axis=0)
        first = jnp.concatenate([parts[1][:cut], parts[1][cut:] + via_second], axis=0)
        return (
            parts[0].astype(jnp.float32)
            + swap(first, "head", 1).astype(jnp.float32)
            + swap(second, "head", 2).astype(jnp.float32)
        )
    bit = size // 2
    while bit:
        parts = [parts[k] + swap(parts[k + bit], "head", bit) for k in range(bit)]
        bit //= 2
    return parts[0].astype(jnp.float32)


def spread(pieces):
    return [pieces[0]] + [swap(pieces[k], "head", k) for k in range(1, len(pieces))]


def attend_kernel(
    spots, latent, up_weight, cosine, sine, keys, values, out_weight, query, mixed, partial, total
):
    block, head = pl.program_id(0), pl.program_id(1)
    count = spots.shape[0] - 2
    rows, width = query.shape
    place = spots[block]
    raw = dot(latent[...], up_weight[...])
    query[...] = rotate(raw, cosine[...], sine[...]).astype(low)
    row = place * rows + lax.broadcasted_iota(jnp.int32, (rows, 1), 0)
    first, second = spots[count], spots[count + 1]
    begin = jnp.where(row >= second, second, jnp.where(row >= first, first, 0))

    def with_keys(size):
        column = lax.broadcasted_iota(jnp.int32, (rows, size), 1)
        scores = dot(query[...], keys[:size], (1, 1)) * (1.0 / math.sqrt(width))
        scores = jnp.where((column <= row) & (column >= begin), scores, masked_value)
        raised = jnp.exp(scores - jnp.max(scores, axis=1, keepdims=True))
        shares = raised * (1.0 / jnp.sum(raised, axis=1, keepdims=True))
        mixed[...] = dot(shares.astype(low), values[:size]).astype(low)

    for number in range(keys.shape[0] // rows):
        pl.when(place == number)(functools.partial(with_keys, (number + 1) * rows))

    product = dot(mixed[...], out_weight[...])

    @pl.when(head == 0)
    def _():
        total[...] = product

    @pl.when(head > 0)
    def _():
        total[...] += product

    @pl.when(head == pl.num_programs(1) - 1)
    def _():
        partial[...] = total[...].astype(low)


def attend(spots, latent, query_up, cosine, sine, keys, values, out_weight):
    total, rank = latent.shape
    spare, head_width = keys.shape
    blocks = spots.shape[0] - 2
    rows = total // blocks
    heads = query_up.shape[1] // head_width
    width = out_weight.shape[1]
    whole = pl.BlockSpec(keys.shape, lambda i, h, s: (0, 0))
    table = pl.BlockSpec((rows, head_width // 2), lambda i, h, s: (i, 0))
    tile = pl.BlockSpec((rows, head_width), lambda i, h, s: (i, h))
    return pl.pallas_call(
        attend_kernel,
        grid_spec=pltpu.PrefetchScalarGridSpec(
            num_scalar_prefetch=1,
            grid=(blocks, heads),
            in_specs=[
                pl.BlockSpec((rows, rank), lambda i, h, s: (i, 0)),
                pl.BlockSpec((rank, head_width), lambda i, h, s: (0, h)),
                table,
                table,
                whole,
                whole,
                pl.BlockSpec((head_width, width), lambda i, h, s: (h, 0)),
            ],
            out_specs=[tile, tile, pl.BlockSpec((rows, width), lambda i, h, s: (i, 0))],
            scratch_shapes=[pltpu.VMEM((rows, width), jnp.float32)],
        ),
        out_shape=[
            jax.ShapeDtypeStruct((total, heads * head_width), low),
            jax.ShapeDtypeStruct((total, heads * head_width), low),
            jax.ShapeDtypeStruct((total, width), low),
        ],
        compiler_params=pltpu.CompilerParams(vmem_limit_bytes=40 << 20),
        cost_estimate=pl.CostEstimate(
            flops=2 * total * heads * head_width * (rank + width + 5 * spare // 4),
            bytes_accessed=2 * total * (rank + width) + blocks * 2 * query_up.size * 3,
            transcendentals=total * heads * spare,
        ),
    )(spots, latent, query_up, cosine, sine, keys, values, out_weight)


def attend_back_kernel(
    spots,
    branch,
    out_weight,
    query,
    keys,
    values,
    up_weight,
    cosine,
    sine,
    key_before,
    value_before,
    query_back,
    partial,
    key_back,
    value_back,
    total,
    grad_query,
):
    block, head = pl.program_id(0), pl.program_id(1)
    count = spots.shape[0] - 2
    rows, width = query.shape
    place = spots[block]
    scale = 1.0 / math.sqrt(width)
    mixed_back = dot(branch[...], out_weight[...], (1, 1)).astype(low)
    column = place * rows + lax.broadcasted_iota(jnp.int32, (1, rows), 1)
    first, second = spots[count], spots[count + 1]
    begin = jnp.where(column >= second, second, jnp.where(column >= first, first, 0))

    @pl.when((block == 0) & (head == 0))
    def _():
        key_back[...] = key_before[...]
        value_back[...] = value_before[...]

    def with_keys(size):
        row = lax.broadcasted_iota(jnp.int32, (size, rows), 0)
        scores = dot(keys[:size], query[...], (1, 1)) * scale
        scores = jnp.where((row <= column) & (row >= begin), scores, masked_value)
        raised = jnp.exp(scores - jnp.max(scores, axis=0, keepdims=True))
        shares = raised * (1.0 / jnp.sum(raised, axis=0, keepdims=True))
        value_back[:size] += dot(shares.astype(low), mixed_back)
        back = dot(values[:size], mixed_back, (1, 1))
        centre = jnp.sum(shares * back, axis=0, keepdims=True)
        scores_back = (shares * (back - centre)).astype(low)
        key_back[:size] += dot(scores_back, query[...]) * scale
        grad_query[...] = dot(scores_back, keys[:size], (0, 0)) * scale

    for number in range(keys.shape[0] // rows):
        pl.when(place == number)(functools.partial(with_keys, (number + 1) * rows))

    turned = rotate(grad_query[...], cosine[...], -sine[...]).astype(low)
    query_back[...] = turned
    product = dot(turned, up_weight[...], (1, 1))

    @pl.when(head == 0)
    def _():
        total[...] = product

    @pl.when(head > 0)
    def _():
        total[...] += product

    @pl.when(head == pl.num_programs(1) - 1)
    def _():
        partial[...] = total[...].astype(low)


def attend_back(
    spots,
    branch,
    out_weight,
    query,
    keys,
    values,
    query_up,
    cosine,
    sine,
    key_before,
    value_before,
):
    total, width = branch.shape
    spare, head_width = keys.shape
    rank = query_up.shape[0]
    blocks = spots.shape[0] - 2
    rows = total // blocks
    heads = query_up.shape[1] // head_width
    whole = pl.BlockSpec(keys.shape, lambda i, h, s: (0, 0))
    table = pl.BlockSpec((rows, head_width // 2), lambda i, h, s: (i, 0))
    tile = pl.BlockSpec((rows, head_width), lambda i, h, s: (i, h))
    return pl.pallas_call(
        attend_back_kernel,
        grid_spec=pltpu.PrefetchScalarGridSpec(
            num_scalar_prefetch=1,
            grid=(blocks, heads),
            in_specs=[
                pl.BlockSpec((rows, width), lambda i, h, s: (i, 0)),
                pl.BlockSpec((head_width, width), lambda i, h, s: (h, 0)),
                tile,
                whole,
                whole,
                pl.BlockSpec((rank, head_width), lambda i, h, s: (0, h)),
                table,
                table,
                whole,
                whole,
            ],
            out_specs=[
                tile,
                pl.BlockSpec((rows, rank), lambda i, h, s: (i, 0)),
                whole,
                whole,
            ],
            scratch_shapes=[
                pltpu.VMEM((rows, rank), jnp.float32),
                pltpu.VMEM((rows, head_width), jnp.float32),
            ],
        ),
        out_shape=[
            jax.ShapeDtypeStruct((total, heads * head_width), low),
            jax.ShapeDtypeStruct((total, rank), low),
            jax.ShapeDtypeStruct(keys.shape, jnp.float32),
            jax.ShapeDtypeStruct(keys.shape, jnp.float32),
        ],
        compiler_params=pltpu.CompilerParams(vmem_limit_bytes=40 << 20),
        cost_estimate=pl.CostEstimate(
            flops=2 * total * heads * head_width * (rank + width + 25 * spare // 8),
            bytes_accessed=2 * total * (rank + width) + blocks * 2 * query_up.size * 3,
            transcendentals=total * heads * spare,
        ),
    )(
        spots,
        branch,
        out_weight,
        query,
        keys,
        values,
        query_up,
        cosine,
        sine,
        key_before,
        value_before,
    )


def after(values, *others):
    return lax.optimization_barrier((values, *others))[0]


def columns_of(weights, feed_part):
    count = lax.axis_size("head")
    me = lax.axis_index("head")
    depth, strip = weights.shape[:2]
    arrived = spread(
        [
            lax.dynamic_slice_in_dim(weights, (me ^ k) * feed_part, feed_part, 2)
            for k in range(count)
        ]
    )
    columns = jnp.zeros((depth, strip * count, feed_part), low)
    for k in range(count):
        columns = lax.dynamic_update_slice(columns, arrived[k], (0, (me ^ k) * strip, 0))
    return columns


def spread_columns(sums, strip):
    count = lax.axis_size("head")
    me = lax.axis_index("head")
    return spread(
        [lax.dynamic_slice_in_dim(sums, (me ^ k) * strip, strip, 1) for k in range(count)]
    )


def placed_columns(arrived, number):
    me = lax.axis_index("head")
    strip, part = arrived[0].shape[1:]
    gradient = jnp.zeros((strip, part * len(arrived)), jnp.float32)
    for k, block in enumerate(arrived):
        gradient = lax.dynamic_update_slice(
            gradient, block[number].astype(jnp.float32), (0, (me ^ k) * part)
        )
    return gradient


def sum_over_batch(values):
    size = lax.axis_size("batch") // 2
    place = lax.axis_index("batch")
    core, line = place & 1, place >> 1
    half = values.shape[0] // 2
    piece = half // size
    given = swap(lax.dynamic_slice_in_dim(values, (1 - core) * half, half), "batch", 1)
    kept = lax.dynamic_slice_in_dim(values, core * half, half) + given
    pieces = [
        lax.dynamic_slice_in_dim(kept, (line ^ k) * piece, piece) for k in range(size)
    ]
    total = pieces[0].astype(jnp.float32)
    for k in range(1, size):
        total = total + swap(pieces[k], "batch", 2 * k).astype(jnp.float32)
    total = total.astype(values.dtype)
    whole = jnp.zeros((half,) + values.shape[1:], values.dtype)
    for k in range(size):
        block = swap(total, "batch", 2 * k) if k else total
        whole = lax.dynamic_update_slice(whole, block, ((line ^ k) * piece, 0))
    return whole


def sum_over_all(values):
    for axis in ("head", "batch"):
        bit = 1
        while bit < lax.axis_size(axis):
            values = values + swap(values, axis, bit)
            bit *= 2
    return values


def widen_kernel(order, block, *outs):
    begin = 0
    for out in outs:
        out[...] = block[:, begin : begin + out.shape[1]].astype(out.dtype)
        begin += out.shape[1]


def widen(order, blocks, widths):
    count = order.shape[0]
    rows = blocks.shape[0] // count
    return pl.pallas_call(
        widen_kernel,
        grid_spec=pltpu.PrefetchScalarGridSpec(
            num_scalar_prefetch=1,
            grid=(count,),
            in_specs=[pl.BlockSpec((rows, blocks.shape[1]), lambda i, order: (order[i], 0))],
            out_specs=[pl.BlockSpec((rows, width), lambda i, order: (i, 0)) for width in widths],
        ),
        out_shape=[
            jax.ShapeDtypeStruct((blocks.shape[0], width), jnp.float32) for width in widths
        ],
        compiler_params=pltpu.CompilerParams(vmem_limit_bytes=24 << 20),
    )(order, blocks)


def shards(
    tokens,
    attention_gain,
    query_down,
    query_gain,
    query_up,
    key_weight,
    value_weight,
    out_weight,
    feed_gain,
    gate_weight,
    up_weight,
    down_weight,
    lengths,
    cotangent,
):
    rows, width = tokens.shape
    count = lax.axis_size("head")
    me = lax.axis_index("head")
    total = rows * count
    head_width = key_weight.shape[1]
    rank = query_up.shape[0]
    feed = gate_weight.shape[1]
    feed_part = feed // count
    strip = gate_weight.shape[0]

    bounds = jnp.cumsum(lengths.reshape(-1), dtype=jnp.int32)
    index = jnp.concatenate(
        [(me ^ k) * rows + jnp.arange(rows, dtype=jnp.int32) for k in range(count)]
    )
    segment = (index >= bounds[0]).astype(jnp.int32) + (index >= bounds[1]).astype(jnp.int32)
    begin = jnp.where(segment == 0, 0, jnp.where(segment == 1, bounds[0], bounds[1]))
    half = head_width // 2
    rates = 10000.0 ** (-2.0 * jnp.arange(half, dtype=jnp.float32) / head_width)
    turns = (index - begin).astype(jnp.float32)[:, None] * rates[None, :]
    cosine, sine = jnp.cos(turns), jnp.sin(turns)
    own_cosine, own_sine = cosine[:rows], sine[:rows]
    ends = bounds[:2]

    def spots(group):
        return jnp.concatenate([me ^ jnp.array(group, jnp.int32), ends])

    def part(values, group):
        return values[group[0] * rows : (group[-1] + 1) * rows]

    groups = sending_order(count)

    def split(values, group):
        return {k: values[i * rows : (i + 1) * rows] for i, k in enumerate(group)}


    inputs = tokens.astype(jnp.float32)
    normed, first_factor = rescale(inputs, attention_gain)
    normed_low = normed.astype(low)
    latent = dot(normed_low, query_down)
    latent_in, latent_factor = rescale(latent, query_gain)
    key_own = rotate(dot(normed_low, key_weight), own_cosine, own_sine).astype(low)
    value_own = dot(normed_low, value_weight).astype(low)
    lkv_own = jnp.concatenate([latent_in.astype(low), key_own, value_own], axis=1)
    gate_up_columns = columns_of(jnp.stack([gate_weight, up_weight]), feed_part)
    gate_up_columns, lkv_own = lax.optimization_barrier((gate_up_columns, lkv_own))
    gate_up_whole = lax.all_gather(gate_up_columns, "batch", axis=1, tiled=True)
    lkv_blocks = gather_near(lkv_own)
    latent_last = lkv_blocks[-1]
    down_columns = columns_of(after(down_weight, latent_last).T[None], feed_part)
    down_whole = lax.all_gather(down_columns[0], "batch", axis=0, tiled=True)
    cotangent_all = jnp.concatenate(gather_near(after(cotangent, latent_last)), axis=0)
    latent_all = jnp.concatenate([block[:, :rank] for block in lkv_blocks], axis=0)
    keys_all, values_all = jnp.zeros((2, total, head_width), low)
    for k in range(count):
        keys_all = lax.dynamic_update_slice(
            keys_all, lkv_blocks[k][:, rank : rank + head_width], ((me ^ k) * rows, 0)
        )
        values_all = lax.dynamic_update_slice(
            values_all, lkv_blocks[k][:, rank + head_width :], ((me ^ k) * rows, 0)
        )
    queries, mixes, partials = {}, {}, {}
    last = cotangent_all
    for group in groups:
        latents = latent_all if len(groups) == 1 else part(latent_all, group)
        latents, last = lax.optimization_barrier((latents, last))
        queries[group[0]], mixes[group[0]], last = attend(
            spots(group),
            latents,
            query_up,
            part(cosine, group),
            part(sine, group),
            keys_all,
            values_all,
            out_weight,
        )
        partials.update(split(last, group))
    attention_part = scatter_near([partials[k] for k in range(count)])
    mixed_low = jnp.concatenate([mixes[group[0]] for group in sorted(groups)], axis=0)
    middle = inputs + attention_part
    inner, second_factor = rescale(middle, feed_gain)
    inner_all = jnp.concatenate(gather_near(inner.astype(low)), axis=0)
    gate_whole, up_whole = gate_up_whole[0], gate_up_whole[1]
    gate = dot(inner_all, gate_whole)
    up = dot(inner_all, up_whole)
    sigma = jax.nn.sigmoid(gate)
    swish = gate * sigma
    hidden_low = (swish * up).astype(low)

    def reduced(left, right):
        return lax.psum_scatter(
            dot(left, right, (0, 0)).astype(low), "batch", scatter_dimension=0, tiled=True
        )

    down_part = dot(cotangent_all, hidden_low, (0, 0)).astype(low)
    down_whole, down_part = lax.optimization_barrier((down_whole, down_part))
    down_sum = lax.psum_scatter(down_part, "batch", scatter_dimension=0, tiled=True)
    grad_hidden = dot(cotangent_all, down_whole)
    slope = sigma * (1.0 + gate * (1.0 - sigma))
    grad_gate_low = (grad_hidden * up * slope).astype(low)
    grad_up_low = (grad_hidden * swish).astype(low)
    grad_inner_partial = (
        dot(grad_gate_low, gate_whole, (1, 1)) + dot(grad_up_low, up_whole, (1, 1))
    ).astype(low)
    gate_part = dot(inner_all, grad_gate_low, (0, 0)).astype(low)
    up_part = dot(inner_all, grad_up_low, (0, 0)).astype(low)
    grad_inner = scatter_near(
        [grad_inner_partial[k * rows : (k + 1) * rows] for k in range(count)]
    )
    grad_inner, gate_part, up_part, hidden_low, down_sum = lax.optimization_barrier(
        (grad_inner, gate_part, up_part, hidden_low, down_sum)
    )
    feed_sum = lax.psum_scatter(
        jnp.concatenate([gate_part, up_part], axis=1), "batch", scatter_dimension=0, tiled=True
    )

    feed_partial = dot(hidden_low, down_whole, (1, 1)).astype(low)
    feed_out = scatter_near([feed_partial[k * rows : (k + 1) * rows] for k in range(count)])
    output = (middle + feed_out).astype(low)

    middle_part, feed_gain_part = rescale_back(middle, second_factor, feed_gain, grad_inner)
    grad_middle = cotangent.astype(jnp.float32) + middle_part
    branch_all = jnp.concatenate(gather_near(grad_middle.astype(low)), axis=0)
    arrived_first = spread_columns(down_sum[None], strip)
    key_grads, value_grads = jnp.zeros((2, total, head_width), jnp.float32)
    query_grads, latent_partials = {}, {}
    for group in groups:
        query_grads[group[0]], last, key_grads, value_grads = attend_back(
            spots(group),
            part(branch_all, group),
            out_weight,
            queries[group[0]],
            keys_all,
            values_all,
            query_up,
            part(cosine, group),
            part(sine, group),
            key_grads,
            value_grads,
        )
        latent_partials.update(split(last, group))
    query_grad_low = jnp.concatenate([query_grads[group[0]] for group in sorted(groups)], axis=0)
    key_value_partials = [
        jnp.concatenate(
            [
                lax.dynamic_slice_in_dim(key_grads, (me ^ k) * rows, rows),
                lax.dynamic_slice_in_dim(value_grads, (me ^ k) * rows, rows),
            ],
            axis=1,
        ).astype(low)
        for k in range(count)
    ]
    query_grad_low, key_value_partials, branch_all, arrived_first, feed_sum = (
        lax.optimization_barrier(
            (query_grad_low, key_value_partials, branch_all, arrived_first, feed_sum)
        )
    )
    latent_back = scatter_near([latent_partials[k] for k in range(count)])
    key_value_back = scatter_near(key_value_partials)
    out_part = dot(mixed_low, branch_all, (0, 0)).astype(low)
    query_part = dot(latent_all, query_grad_low, (0, 0)).astype(low)
    query_up_gradient, out_gradient = lax.psum((query_part, out_part), "batch")
    latent_grad, query_gain_part = rescale_back(latent, latent_factor, query_gain, latent_back)
    key_back = rotate_back(key_value_back[:, :head_width], own_cosine, own_sine)
    lkv_grad_low = jnp.concatenate(
        [latent_grad, key_back, key_value_back[:, head_width:]], axis=1
    ).astype(low)

    slice_width = width // count
    normed_slices = jnp.concatenate(
        spread(
            [
                lax.dynamic_slice_in_dim(normed_low, (me ^ k) * slice_width, slice_width, 1)
                for k in range(count)
            ]
        ),
        axis=0,
    )
    lkv_grad_all = jnp.concatenate(gather_near(lkv_grad_low), axis=0)
    shared_part = dot(normed_slices, lkv_grad_all, (0, 0)).astype(low)
    grad_normed = (
        dot(lkv_grad_low[:, :rank], query_down, (1, 1))
        + dot(lkv_grad_low[:, rank : rank + head_width], key_weight, (1, 1))
        + dot(lkv_grad_low[:, rank + head_width :], value_weight, (1, 1))
    )
    input_part, attention_gain_part = rescale_back(
        inputs, first_factor, attention_gain, grad_normed
    )
    input_gradient = grad_middle + input_part
    gains = sum_over_all(
        jnp.concatenate([attention_gain_part, feed_gain_part, query_gain_part]).reshape(-1, 128)
    ).reshape(-1)
    arrived_second = spread_columns(
        jnp.stack(jnp.split(after(feed_sum, shared_part), 2, axis=1)), strip
    )
    shared_half = sum_over_batch(shared_part)
    blocks = gather_near(shared_half)
    mine = jnp.concatenate(blocks + [swap(block, "batch", 1) for block in blocks], axis=0)
    spot = jnp.arange(2 * count, dtype=jnp.int32)
    order = ((spot >> 1) ^ me) + count * ((spot & 1) ^ (lax.axis_index("batch") & 1))
    query_down_gradient, key_gradient, value_gradient = widen(
        order, mine, (rank, head_width, head_width)
    )
    return (
        output,
        input_gradient,
        gains[:width],
        query_down_gradient,
        gains[2 * width :],
        query_up_gradient.astype(jnp.float32),
        key_gradient,
        value_gradient,
        out_gradient.astype(jnp.float32),
        gains[width : 2 * width],
        placed_columns(arrived_second, 0),
        placed_columns(arrived_second, 1),
        placed_columns(arrived_first, 0).T,
    )


def solution(mesh):
    rows = P(("batch", "head"), None)
    columns = P(None, ("batch", "head"))
    return jax.shard_map(
        shards,
        mesh=mesh,
        in_specs=(
            rows,
            P(),
            P(),
            P(),
            P(None, "head"),
            P(),
            P(),
            P("head", None),
            P(),
            rows,
            rows,
            columns,
            P("batch", None),
            rows,
        ),
        out_specs=(
            rows,
            rows,
            P(),
            P(),
            P(),
            P(None, "head"),
            P(),
            P(),
            P("head", None),
            P(),
            rows,
            rows,
            columns,
        ),
        check_vma=False,
    )
```

```python
import functools
import math

import jax
import jax.numpy as jnp
from jax import lax
from jax.experimental import pallas as pl
from jax.experimental.pallas import tpu as pltpu
from jax.sharding import PartitionSpec as P

epsilon = 1e-05
masked_value = -1e30
low = jnp.bfloat16


def dot(left, right, contract=(1, 0)):
    return lax.dot_general(
        left,
        right,
        (((contract[0],), (contract[1],)), ((), ())),
        preferred_element_type=jnp.float32,
    )


def rescale(values, gain):
    factor = lax.rsqrt(jnp.mean(values * values, axis=-1, keepdims=True) + epsilon)
    return (values * factor * gain, factor)


def rescale_back(values, factor, gain, upstream):
    weighted = upstream * gain
    inner_mean = jnp.mean(values * weighted, axis=-1, keepdims=True)
    back = factor * weighted - values * (factor * factor * factor) * inner_mean
    return (back, jnp.sum(upstream * values * factor, axis=0))


def rotate(values, cosine, sine):
    half = values.shape[-1] // 2
    first = values[..., :half]
    second = values[..., half:]
    return jnp.concatenate(
        [first * cosine - second * sine, second * cosine + first * sine], axis=-1
    )


def rotate_back(grads, cosine, sine):
    return rotate(grads, cosine, -sine)


def swap(values, axis, bit):
    size = lax.axis_size(axis)
    return lax.ppermute(values, axis, [(i, i ^ bit) for i in range(size)])


def after(values, *others):
    return lax.optimization_barrier((values, *others))[0] if others else values


def sending_order(size):
    if size == 4:
        return [[3], [1, 2], [0]]
    return [list(range(size))]


def gather_begin(own):
    if lax.axis_size("head") == 4:
        return swap(own, "head", 1), swap(own, "head", 2)
    return ()


def gather_end(own, begun):
    size = lax.axis_size("head")
    if size == 4:
        cut = own.shape[0] // 2
        first, second = begun
        third = jnp.concatenate(
            [swap(first[:cut], "head", 2), swap(second[cut:], "head", 1)], axis=0
        )
        return [own, first, second, third]
    blocks = [own]
    bit = 1
    while bit < size:
        blocks = blocks + [swap(block, "head", bit) for block in blocks]
        bit *= 2
    return blocks


def gather_near(own, *beside):
    return gather_end(own, tuple(after(block, *beside) for block in gather_begin(own)))


def scatter_near(compute, groups):
    size = lax.axis_size("head")
    if size == 4:
        parts = dict(zip(groups[0], compute(groups[0], ())))
        cut = parts[3].shape[0] // 2
        via_first = swap(parts[3][:cut], "head", 1)
        via_second = swap(parts[3][cut:], "head", 2)
        parts.update(zip(groups[1], compute(groups[1], (parts[3],))))
        second = jnp.concatenate([parts[2][:cut] + via_first, parts[2][cut:]], axis=0)
        first = jnp.concatenate([parts[1][:cut], parts[1][cut:] + via_second], axis=0)
        if len(groups) > 2:
            parts.update(zip(groups[2], compute(groups[2], (first, second))))
        return (
            parts[0].astype(jnp.float32)
            + swap(first, "head", 1).astype(jnp.float32)
            + swap(second, "head", 2).astype(jnp.float32)
        ), (first, second)
    parts = compute(list(range(size)), ())
    begun = tuple(parts)
    bit = size // 2
    while bit:
        parts = [parts[k] + swap(parts[k + bit], "head", bit) for k in range(bit)]
        bit //= 2
    return parts[0].astype(jnp.float32), begun


def spread(pieces):
    return [pieces[0]] + [swap(pieces[k], "head", k) for k in range(1, len(pieces))]


def attend_kernel(
    spots, latent, up_weight, cosine, sine, keys, values, out_weight, query, mixed, partial, total
):
    block, head = pl.program_id(0), pl.program_id(1)
    count = spots.shape[0] - 2
    rows, width = query.shape
    place = spots[block]
    raw = dot(latent[...], up_weight[...])
    query[...] = rotate(raw, cosine[...], sine[...]).astype(low)
    row = place * rows + lax.broadcasted_iota(jnp.int32, (rows, 1), 0)
    first, second = spots[count], spots[count + 1]
    begin = jnp.where(row >= second, second, jnp.where(row >= first, first, 0))

    def with_keys(size):
        column = lax.broadcasted_iota(jnp.int32, (rows, size), 1)
        scores = dot(query[...], keys[:size], (1, 1)) * (1.0 / math.sqrt(width))
        scores = jnp.where((column <= row) & (column >= begin), scores, masked_value)
        raised = jnp.exp(scores - jnp.max(scores, axis=1, keepdims=True))
        shares = raised * (1.0 / jnp.sum(raised, axis=1, keepdims=True))
        mixed[...] = dot(shares.astype(low), values[:size]).astype(low)

    for number in range(keys.shape[0] // rows):
        pl.when(place == number)(functools.partial(with_keys, (number + 1) * rows))

    product = dot(mixed[...], out_weight[...])

    @pl.when(head == 0)
    def _():
        total[...] = product

    @pl.when(head > 0)
    def _():
        total[...] += product

    @pl.when(head == pl.num_programs(1) - 1)
    def _():
        partial[...] = total[...].astype(low)


def attend(spots, latent, query_up, cosine, sine, keys, values, out_weight):
    total, rank = latent.shape
    spare, head_width = keys.shape
    blocks = spots.shape[0] - 2
    rows = total // blocks
    heads = query_up.shape[1] // head_width
    width = out_weight.shape[1]
    whole = pl.BlockSpec(keys.shape, lambda i, h, s: (0, 0))
    table = pl.BlockSpec((rows, head_width // 2), lambda i, h, s: (i, 0))
    tile = pl.BlockSpec((rows, head_width), lambda i, h, s: (i, h))
    return pl.pallas_call(
        attend_kernel,
        grid_spec=pltpu.PrefetchScalarGridSpec(
            num_scalar_prefetch=1,
            grid=(blocks, heads),
            in_specs=[
                pl.BlockSpec((rows, rank), lambda i, h, s: (i, 0)),
                pl.BlockSpec((rank, head_width), lambda i, h, s: (0, h)),
                table,
                table,
                whole,
                whole,
                pl.BlockSpec((head_width, width), lambda i, h, s: (h, 0)),
            ],
            out_specs=[tile, tile, pl.BlockSpec((rows, width), lambda i, h, s: (i, 0))],
            scratch_shapes=[pltpu.VMEM((rows, width), jnp.float32)],
        ),
        out_shape=[
            jax.ShapeDtypeStruct((total, heads * head_width), low),
            jax.ShapeDtypeStruct((total, heads * head_width), low),
            jax.ShapeDtypeStruct((total, width), low),
        ],
        compiler_params=pltpu.CompilerParams(vmem_limit_bytes=40 << 20),
        cost_estimate=pl.CostEstimate(
            flops=2 * total * heads * head_width * (rank + width + 5 * spare // 4),
            bytes_accessed=2 * total * (rank + width) + blocks * 2 * query_up.size * 3,
            transcendentals=total * heads * spare,
        ),
    )(spots, latent, query_up, cosine, sine, keys, values, out_weight)


def attend_back_kernel(
    spots,
    branch,
    out_weight,
    query,
    keys,
    values,
    up_weight,
    cosine,
    sine,
    key_before,
    value_before,
    query_back,
    partial,
    key_back,
    value_back,
    total,
    grad_query,
):
    block, head = pl.program_id(0), pl.program_id(1)
    count = spots.shape[0] - 2
    rows, width = query.shape
    place = spots[block]
    scale = 1.0 / math.sqrt(width)
    mixed_back = dot(branch[...], out_weight[...], (1, 1)).astype(low)
    column = place * rows + lax.broadcasted_iota(jnp.int32, (1, rows), 1)
    first, second = spots[count], spots[count + 1]
    begin = jnp.where(column >= second, second, jnp.where(column >= first, first, 0))

    @pl.when((block == 0) & (head == 0))
    def _():
        key_back[...] = key_before[...]
        value_back[...] = value_before[...]

    def with_keys(size):
        row = lax.broadcasted_iota(jnp.int32, (size, rows), 0)
        scores = dot(keys[:size], query[...], (1, 1)) * scale
        scores = jnp.where((row <= column) & (row >= begin), scores, masked_value)
        raised = jnp.exp(scores - jnp.max(scores, axis=0, keepdims=True))
        shares = raised * (1.0 / jnp.sum(raised, axis=0, keepdims=True))
        value_back[:size] += dot(shares.astype(low), mixed_back)
        back = dot(values[:size], mixed_back, (1, 1))
        centre = jnp.sum(shares * back, axis=0, keepdims=True)
        scores_back = (shares * (back - centre)).astype(low)
        key_back[:size] += dot(scores_back, query[...]) * scale
        grad_query[...] = dot(scores_back, keys[:size], (0, 0)) * scale

    for number in range(keys.shape[0] // rows):
        pl.when(place == number)(functools.partial(with_keys, (number + 1) * rows))

    turned = rotate(grad_query[...], cosine[...], -sine[...]).astype(low)
    query_back[...] = turned
    product = dot(turned, up_weight[...], (1, 1))

    @pl.when(head == 0)
    def _():
        total[...] = product

    @pl.when(head > 0)
    def _():
        total[...] += product

    @pl.when(head == pl.num_programs(1) - 1)
    def _():
        partial[...] = total[...].astype(low)


def attend_back(
    spots,
    branch,
    out_weight,
    query,
    keys,
    values,
    query_up,
    cosine,
    sine,
    key_before,
    value_before,
):
    total, width = branch.shape
    spare, head_width = keys.shape
    rank = query_up.shape[0]
    blocks = spots.shape[0] - 2
    rows = total // blocks
    heads = query_up.shape[1] // head_width
    whole = pl.BlockSpec(keys.shape, lambda i, h, s: (0, 0))
    table = pl.BlockSpec((rows, head_width // 2), lambda i, h, s: (i, 0))
    tile = pl.BlockSpec((rows, head_width), lambda i, h, s: (i, h))
    return pl.pallas_call(
        attend_back_kernel,
        grid_spec=pltpu.PrefetchScalarGridSpec(
            num_scalar_prefetch=1,
            grid=(blocks, heads),
            in_specs=[
                pl.BlockSpec((rows, width), lambda i, h, s: (i, 0)),
                pl.BlockSpec((head_width, width), lambda i, h, s: (h, 0)),
                tile,
                whole,
                whole,
                pl.BlockSpec((rank, head_width), lambda i, h, s: (0, h)),
                table,
                table,
                whole,
                whole,
            ],
            out_specs=[
                tile,
                pl.BlockSpec((rows, rank), lambda i, h, s: (i, 0)),
                whole,
                whole,
            ],
            scratch_shapes=[
                pltpu.VMEM((rows, rank), jnp.float32),
                pltpu.VMEM((rows, head_width), jnp.float32),
            ],
        ),
        out_shape=[
            jax.ShapeDtypeStruct((total, heads * head_width), low),
            jax.ShapeDtypeStruct((total, rank), low),
            jax.ShapeDtypeStruct(keys.shape, jnp.float32),
            jax.ShapeDtypeStruct(keys.shape, jnp.float32),
        ],
        compiler_params=pltpu.CompilerParams(vmem_limit_bytes=40 << 20),
        cost_estimate=pl.CostEstimate(
            flops=2 * total * heads * head_width * (rank + width + 25 * spare // 8),
            bytes_accessed=2 * total * (rank + width) + blocks * 2 * query_up.size * 3,
            transcendentals=total * heads * spare,
        ),
    )(
        spots,
        branch,
        out_weight,
        query,
        keys,
        values,
        query_up,
        cosine,
        sine,
        key_before,
        value_before,
    )


def feed_kernel(order, inner, weights, *refs):
    hidden, by_up, by_gate = refs[-3:]
    gate = dot(inner[...], weights[0])
    sigma = 1.0 / (1.0 + jnp.exp(-gate))
    swish = gate * sigma
    up = dot(inner[...], weights[1])
    hidden[...] = (swish * up).astype(low)
    by_gate[...] = swish.astype(low)
    by_up[...] = (up * (sigma * (1.0 + gate * (1.0 - sigma)))).astype(low)


def feed(inner, weights, group, count, earlier):
    rows = inner.shape[0] // len(group)
    width = inner.shape[1]
    part = weights.shape[2]
    shape = jax.ShapeDtypeStruct((rows * count, part), low)
    return pl.pallas_call(
        feed_kernel,
        grid_spec=pltpu.PrefetchScalarGridSpec(
            num_scalar_prefetch=1,
            grid=(len(group),),
            in_specs=[
                pl.BlockSpec((rows, width), lambda i, order: (i, 0)),
                pl.BlockSpec(
                    weights.shape, lambda i, order: (0, 0, 0), pipeline_mode=pl.Buffered(1)
                ),
            ]
            + [pl.BlockSpec(memory_space=pl.ANY)] * len(earlier),
            out_specs=[pl.BlockSpec((rows, part), lambda i, order: (order[i], 0))] * 3,
        ),
        out_shape=[shape, shape, shape],
        input_output_aliases={3 + i: i for i in range(len(earlier))},
        compiler_params=pltpu.CompilerParams(vmem_limit_bytes=40 << 20),
        cost_estimate=pl.CostEstimate(
            flops=4 * inner.size * part,
            bytes_accessed=2 * rows * len(group) * (width + 3 * part) + 2 * weights.size,
            transcendentals=rows * len(group) * part,
        ),
    )(jnp.array(group, jnp.int32), inner, weights, *earlier)


def feed_back_kernel(order, cotangent, down, weights, by_up, by_gate, *refs):
    grads, partial = refs[-2:]
    back = dot(cotangent[...], down[...])
    grad_gate = (back * by_up[...].astype(jnp.float32)).astype(low)
    grad_up = (back * by_gate[...].astype(jnp.float32)).astype(low)
    grads[0] = grad_gate
    grads[1] = grad_up
    partial[...] = (
        dot(grad_gate, weights[0], (1, 1)) + dot(grad_up, weights[1], (1, 1))
    ).astype(low)


def feed_back(cotangent, down, weights, by_up, by_gate, group, count, earlier):
    total, width = cotangent.shape
    rows = total // count
    part = weights.shape[2]
    tile = pl.BlockSpec((rows, part), lambda i, order: (order[i], 0))
    return pl.pallas_call(
        feed_back_kernel,
        grid_spec=pltpu.PrefetchScalarGridSpec(
            num_scalar_prefetch=1,
            grid=(len(group),),
            in_specs=[
                pl.BlockSpec((rows, width), lambda i, order: (order[i], 0)),
                pl.BlockSpec(down.shape, lambda i, order: (0, 0), pipeline_mode=pl.Buffered(1)),
                pl.BlockSpec(
                    weights.shape, lambda i, order: (0, 0, 0), pipeline_mode=pl.Buffered(1)
                ),
                tile,
                tile,
            ]
            + [pl.BlockSpec(memory_space=pl.ANY)] * len(earlier),
            out_specs=[
                pl.BlockSpec((2, rows, part), lambda i, order: (0, order[i], 0)),
                pl.BlockSpec((rows, width), lambda i, order: (i, 0)),
            ],
        ),
        out_shape=[
            jax.ShapeDtypeStruct((2, total, part), low),
            jax.ShapeDtypeStruct((rows * len(group), width), low),
        ],
        input_output_aliases={6 + i: i for i in range(len(earlier))},
        compiler_params=pltpu.CompilerParams(vmem_limit_bytes=48 << 20),
        cost_estimate=pl.CostEstimate(
            flops=6 * rows * len(group) * width * part,
            bytes_accessed=4 * rows * len(group) * (width + 2 * part) + 6 * down.size,
            transcendentals=0,
        ),
    )(jnp.array(group, jnp.int32), cotangent, down, weights, by_up, by_gate, *earlier)


def weight_kernel(left, right, out):
    out[0] = dot(left[...], right[0], (0, 0)).astype(low)


def weight_terms(left, right):
    total, width = left.shape
    number, spare, part = right.shape
    strip = width // lax.axis_size("batch")
    return pl.pallas_call(
        weight_kernel,
        grid=(number, width // strip),
        in_specs=[
            pl.BlockSpec((total, strip), lambda g, i: (0, i)),
            pl.BlockSpec((1, total, part), lambda g, i: (g, 0, 0)),
        ],
        out_specs=pl.BlockSpec((1, strip, part), lambda g, i: (g, i, 0)),
        out_shape=jax.ShapeDtypeStruct((number, width, part), low),
        compiler_params=pltpu.CompilerParams(vmem_limit_bytes=40 << 20),
        cost_estimate=pl.CostEstimate(
            flops=2 * number * total * width * part,
            bytes_accessed=2 * total * (width + number * part) + 2 * number * width * part,
            transcendentals=0,
        ),
    )(left, right)


def sum_over_batch_rows(values):
    return lax.psum_scatter(values, "batch", scatter_dimension=1, tiled=True)


def columns_of(weights, feed_part):
    count = lax.axis_size("head")
    me = lax.axis_index("head")
    depth, strip = weights.shape[:2]
    arrived = spread(
        [
            lax.dynamic_slice_in_dim(weights, (me ^ k) * feed_part, feed_part, 2)
            for k in range(count)
        ]
    )
    columns = jnp.zeros((depth, strip * count, feed_part), low)
    for k in range(count):
        columns = lax.dynamic_update_slice(columns, arrived[k], (0, (me ^ k) * strip, 0))
    return columns


def spread_columns(sums, strip):
    count = lax.axis_size("head")
    me = lax.axis_index("head")
    return spread(
        [lax.dynamic_slice_in_dim(sums, (me ^ k) * strip, strip, 1) for k in range(count)]
    )


def placed_columns(arrived, number):
    me = lax.axis_index("head")
    strip, part = arrived[0].shape[1:]
    gradient = jnp.zeros((strip, part * len(arrived)), jnp.float32)
    for k, block in enumerate(arrived):
        gradient = lax.dynamic_update_slice(
            gradient, block[number].astype(jnp.float32), (0, (me ^ k) * part)
        )
    return gradient


def sum_over_batch(values):
    size = lax.axis_size("batch") // 2
    place = lax.axis_index("batch")
    core, line = place & 1, place >> 1
    half = values.shape[0] // 2
    piece = half // size
    given = swap(lax.dynamic_slice_in_dim(values, (1 - core) * half, half), "batch", 1)
    kept = lax.dynamic_slice_in_dim(values, core * half, half) + given
    pieces = [
        lax.dynamic_slice_in_dim(kept, (line ^ k) * piece, piece) for k in range(size)
    ]
    total = pieces[0].astype(jnp.float32)
    for k in range(1, size):
        total = total + swap(pieces[k], "batch", 2 * k).astype(jnp.float32)
    total = total.astype(values.dtype)
    whole = jnp.zeros((half,) + values.shape[1:], values.dtype)
    for k in range(size):
        block = swap(total, "batch", 2 * k) if k else total
        whole = lax.dynamic_update_slice(whole, block, ((line ^ k) * piece, 0))
    return whole


def sum_over_all(values):
    for axis in ("head", "batch"):
        bit = 1
        while bit < lax.axis_size(axis):
            values = values + swap(values, axis, bit)
            bit *= 2
    return values


def widen_kernel(order, block, *outs):
    begin = 0
    for out in outs:
        out[...] = block[:, begin : begin + out.shape[1]].astype(out.dtype)
        begin += out.shape[1]


def widen(order, blocks, widths):
    count = order.shape[0]
    rows = blocks.shape[0] // count
    return pl.pallas_call(
        widen_kernel,
        grid_spec=pltpu.PrefetchScalarGridSpec(
            num_scalar_prefetch=1,
            grid=(count,),
            in_specs=[pl.BlockSpec((rows, blocks.shape[1]), lambda i, order: (order[i], 0))],
            out_specs=[pl.BlockSpec((rows, width), lambda i, order: (i, 0)) for width in widths],
        ),
        out_shape=[
            jax.ShapeDtypeStruct((blocks.shape[0], width), jnp.float32) for width in widths
        ],
        compiler_params=pltpu.CompilerParams(vmem_limit_bytes=24 << 20),
    )(order, blocks)


def shards(
    tokens,
    attention_gain,
    query_down,
    query_gain,
    query_up,
    key_weight,
    value_weight,
    out_weight,
    feed_gain,
    gate_weight,
    up_weight,
    down_weight,
    lengths,
    cotangent,
):
    rows, width = tokens.shape
    count = lax.axis_size("head")
    me = lax.axis_index("head")
    total = rows * count
    head_width = key_weight.shape[1]
    rank = query_up.shape[0]
    feed_part = gate_weight.shape[1] // count
    strip = gate_weight.shape[0]

    bounds = jnp.cumsum(lengths.reshape(-1), dtype=jnp.int32)
    index = jnp.concatenate(
        [(me ^ k) * rows + jnp.arange(rows, dtype=jnp.int32) for k in range(count)]
    )
    segment = (index >= bounds[0]).astype(jnp.int32) + (index >= bounds[1]).astype(jnp.int32)
    begin = jnp.where(segment == 0, 0, jnp.where(segment == 1, bounds[0], bounds[1]))
    half = head_width // 2
    rates = 10000.0 ** (-2.0 * jnp.arange(half, dtype=jnp.float32) / head_width)
    turns = (index - begin).astype(jnp.float32)[:, None] * rates[None, :]
    cosine, sine = jnp.cos(turns), jnp.sin(turns)
    own_cosine, own_sine = cosine[:rows], sine[:rows]
    ends = bounds[:2]

    def spots(group):
        return jnp.concatenate([me ^ jnp.array(group, jnp.int32), ends])

    def part(values, group):
        return values[group[0] * rows : (group[-1] + 1) * rows]

    groups = sending_order(count)

    def split(values, group):
        return [values[i * rows : (i + 1) * rows] for i in range(len(group))]


    inputs = tokens.astype(jnp.float32)
    normed, first_factor = rescale(inputs, attention_gain)
    normed_low = normed.astype(low)
    latent = dot(normed_low, query_down)
    latent_in, latent_factor = rescale(latent, query_gain)
    key_own = rotate(dot(normed_low, key_weight), own_cosine, own_sine).astype(low)
    value_own = dot(normed_low, value_weight).astype(low)
    lkv_own = jnp.concatenate([latent_in.astype(low), key_own, value_own], axis=1)
    gate_up_columns = columns_of(jnp.stack([gate_weight, up_weight]), feed_part)
    gate_up_columns = after(gate_up_columns, lkv_own)
    gate_up_whole = lax.all_gather(gate_up_columns, "batch", axis=1, tiled=True)
    lkv_blocks = gather_near(lkv_own, gate_up_columns)
    latent_last = lkv_blocks[-1]
    down_columns = columns_of(after(down_weight, latent_last).T[None], feed_part)
    latent_all = jnp.concatenate([block[:, :rank] for block in lkv_blocks], axis=0)
    keys_all, values_all = jnp.zeros((2, total, head_width), low)
    for k in range(count):
        keys_all = lax.dynamic_update_slice(
            keys_all, lkv_blocks[k][:, rank : rank + head_width], ((me ^ k) * rows, 0)
        )
        values_all = lax.dynamic_update_slice(
            values_all, lkv_blocks[k][:, rank + head_width :], ((me ^ k) * rows, 0)
        )
    queries, mixes = {}, {}
    cotangent_begun = gather_begin(after(cotangent, latent_last))

    def attention(group, tie):
        if group == [0]:
            tie += cotangent_begun
        queries[group[0]], mixes[group[0]], partial = attend(
            spots(group),
            after(part(latent_all, group), *tie),
            query_up,
            part(cosine, group),
            part(sine, group),
            keys_all,
            values_all,
            out_weight,
        )
        return split(partial, group)

    attention_part, _ = scatter_near(attention, groups)
    mixed_low = jnp.concatenate([mixes[group[0]] for group in sorted(groups)], axis=0)
    middle = inputs + attention_part
    inner, second_factor = rescale(middle, feed_gain)
    inner_low = inner.astype(low)
    down_whole = lax.all_gather(after(down_columns[0], inner_low), "batch", axis=0, tiled=True)
    found = []

    def forward(blocks, group, *tie):
        rows_in = after(jnp.concatenate(blocks, axis=0), *tie)
        found[:] = feed(rows_in, gate_up_whole, group, count, list(found))

    if count == 4:
        begun = gather_begin(inner_low)
        forward([inner_low], [0])
        inner_blocks = gather_end(inner_low, tuple(after(block, found[0]) for block in begun))
        forward(inner_blocks[1:3], [1, 2])
        forward(inner_blocks[3:], [3])
        cotangent_begun = tuple(after(block, inner_blocks[3]) for block in cotangent_begun)
    else:
        inner_blocks = gather_near(inner_low)
        forward(inner_blocks, list(range(count)))
    cotangent_all = jnp.concatenate(gather_end(cotangent, cotangent_begun), axis=0)
    hidden_low, by_up, by_gate = found
    inner_all = jnp.concatenate(inner_blocks, axis=0)
    down_terms = weight_terms(cotangent_all, hidden_low[None])
    down_terms, by_up = lax.optimization_barrier((down_terms, by_up))
    down_sum = sum_over_batch_rows(down_terms)[0]
    found = []
    slice_width = width // count
    normed_later = after(normed_low, down_terms)
    normed_slices = spread(
        [
            lax.dynamic_slice_in_dim(normed_later, (me ^ k) * slice_width, slice_width, 1)
            for k in range(count)
        ]
    )

    def back(group, tie):
        if tie:
            tie += tuple(normed_slices)
        grads, partial = feed_back(
            cotangent_all,
            after(down_whole, *tie),
            gate_up_whole,
            by_up,
            by_gate,
            group,
            count,
            list(found),
        )
        found[:] = [grads]
        return split(partial, group)

    grad_inner, begun = scatter_near(
        back, [groups[0], sum(groups[1:], [])] if len(groups) > 1 else groups
    )
    feed_terms = weight_terms(inner_all, after(found[0], *begun))
    grad_inner, feed_terms, down_sum = lax.optimization_barrier(
        (grad_inner, feed_terms, down_sum)
    )
    feed_sum = sum_over_batch_rows(feed_terms)

    middle_part, feed_gain_part = rescale_back(middle, second_factor, feed_gain, grad_inner)
    grad_middle = cotangent.astype(jnp.float32) + middle_part
    branch_low = grad_middle.astype(low)
    branch_all = jnp.concatenate(gather_near(branch_low), axis=0)
    feed_partial = dot(after(hidden_low, branch_low), down_whole, (1, 1)).astype(low)
    branch_all, feed_partial, down_sum = lax.optimization_barrier(
        (branch_all, feed_partial, down_sum)
    )
    arrived_first = spread_columns(down_sum[None], strip)
    key_grads, value_grads = jnp.zeros((2, total, head_width), jnp.float32)
    query_grads = {}
    totals = [key_grads, value_grads]

    def attention_back(group, tie):
        query_grads[group[0]], partial, totals[0], totals[1] = attend_back(
            spots(group),
            after(part(branch_all, group), *tie),
            out_weight,
            queries[group[0]],
            keys_all,
            values_all,
            query_up,
            part(cosine, group),
            part(sine, group),
            *totals,
        )
        return split(partial, group)

    latent_back, _ = scatter_near(attention_back, groups)
    key_grads, value_grads = totals
    query_grad_low = jnp.concatenate([query_grads[group[0]] for group in sorted(groups)], axis=0)
    key_value_partials = [
        jnp.concatenate(
            [
                lax.dynamic_slice_in_dim(key_grads, (me ^ k) * rows, rows),
                lax.dynamic_slice_in_dim(value_grads, (me ^ k) * rows, rows),
            ],
            axis=1,
        ).astype(low)
        for k in range(count)
    ]
    out_part = dot(mixed_low, branch_all, (0, 0)).astype(low)
    query_part = dot(latent_all, query_grad_low, (0, 0)).astype(low)
    query_part, out_part, key_value_partials, arrived_first, feed_sum = (
        lax.optimization_barrier(
            (query_part, out_part, key_value_partials, arrived_first, feed_sum)
        )
    )
    key_value_back, _ = scatter_near(
        lambda group, tie: [key_value_partials[k] for k in group], groups
    )
    query_up_gradient, out_gradient = lax.psum((query_part, out_part), "batch")
    latent_grad, query_gain_part = rescale_back(latent, latent_factor, query_gain, latent_back)
    key_back = rotate_back(key_value_back[:, :head_width], own_cosine, own_sine)
    lkv_grad_low = jnp.concatenate(
        [latent_grad, key_back, key_value_back[:, head_width:]], axis=1
    ).astype(low)

    lkv_grad_all = jnp.concatenate(gather_near(lkv_grad_low), axis=0)
    shared_part = dot(jnp.concatenate(normed_slices, axis=0), lkv_grad_all, (0, 0)).astype(low)
    feed_partial = after(feed_partial, shared_part)
    feed_out, _ = scatter_near(
        lambda group, tie: split(part(feed_partial, group), group), groups
    )
    output = (middle + feed_out).astype(low)

    grad_normed = (
        dot(lkv_grad_low[:, :rank], query_down, (1, 1))
        + dot(lkv_grad_low[:, rank : rank + head_width], key_weight, (1, 1))
        + dot(lkv_grad_low[:, rank + head_width :], value_weight, (1, 1))
    )
    input_part, attention_gain_part = rescale_back(
        inputs, first_factor, attention_gain, grad_normed
    )
    input_gradient = grad_middle + input_part
    gains = sum_over_all(
        jnp.concatenate([attention_gain_part, feed_gain_part, query_gain_part]).reshape(-1, 128)
    ).reshape(-1)
    arrived_second = spread_columns(after(feed_sum, shared_part), strip)
    shared_half = sum_over_batch(shared_part)
    blocks = gather_near(shared_half)
    blocks, query_up_gradient, out_gradient = lax.optimization_barrier(
        (blocks, query_up_gradient, out_gradient)
    )
    mine = jnp.concatenate(blocks + [swap(block, "batch", 1) for block in blocks], axis=0)
    spot = jnp.arange(2 * count, dtype=jnp.int32)
    order = ((spot >> 1) ^ me) + count * ((spot & 1) ^ (lax.axis_index("batch") & 1))
    query_down_gradient, key_gradient, value_gradient = widen(
        order, mine, (rank, head_width, head_width)
    )
    return (
        output,
        input_gradient,
        gains[:width],
        query_down_gradient,
        gains[2 * width :],
        query_up_gradient.astype(jnp.float32),
        key_gradient,
        value_gradient,
        out_gradient.astype(jnp.float32),
        gains[width : 2 * width],
        placed_columns(arrived_second, 0),
        placed_columns(arrived_second, 1),
        placed_columns(arrived_first, 0).T,
    )


def solution(mesh):
    rows = P(("batch", "head"), None)
    columns = P(None, ("batch", "head"))
    return jax.shard_map(
        shards,
        mesh=mesh,
        in_specs=(
            rows,
            P(),
            P(),
            P(),
            P(None, "head"),
            P(),
            P(),
            P("head", None),
            P(),
            rows,
            rows,
            columns,
            P("batch", None),
            rows,
        ),
        out_specs=(
            rows,
            rows,
            P(),
            P(),
            P(),
            P(None, "head"),
            P(),
            P(),
            P("head", None),
            P(),
            rows,
            rows,
            columns,
        ),
        check_vma=False,
    )
```

```python
import functools
import math

import jax
import jax.numpy as jnp
from jax import lax
from jax.experimental import pallas as pl
from jax.experimental.pallas import tpu as pltpu
from jax.sharding import PartitionSpec as P

epsilon = 1e-05
masked_value = -1e30
low = jnp.bfloat16


def dot(left, right, contract=(1, 0)):
    return lax.dot_general(
        left,
        right,
        (((contract[0],), (contract[1],)), ((), ())),
        preferred_element_type=jnp.float32,
    )


def rescale(values, gain):
    factor = lax.rsqrt(jnp.mean(values * values, axis=-1, keepdims=True) + epsilon)
    return (values * factor * gain, factor)


def rescale_back(values, factor, gain, upstream):
    weighted = upstream * gain
    inner_mean = jnp.mean(values * weighted, axis=-1, keepdims=True)
    back = factor * weighted - values * (factor * factor * factor) * inner_mean
    return (back, jnp.sum(upstream * values * factor, axis=0))


def rotate(values, cosine, sine):
    half = values.shape[-1] // 2
    first = values[..., :half]
    second = values[..., half:]
    return jnp.concatenate(
        [first * cosine - second * sine, second * cosine + first * sine], axis=-1
    )


def rotate_back(grads, cosine, sine):
    return rotate(grads, cosine, -sine)


def swap(values, axis, bit):
    size = lax.axis_size(axis)
    return lax.ppermute(values, axis, [(i, i ^ bit) for i in range(size)])


def after(values, *others):
    return lax.optimization_barrier((values, *others))[0] if others else values


def sending_order(size):
    if size == 4:
        return [[3], [1, 2], [0]]
    return [list(range(size))]


def gather_begin(own):
    if lax.axis_size("head") == 4:
        return swap(own, "head", 1), swap(own, "head", 2)
    return ()


def gather_end(own, begun):
    size = lax.axis_size("head")
    if size == 4:
        cut = own.shape[0] // 2
        first, second = begun
        third = jnp.concatenate(
            [swap(first[:cut], "head", 2), swap(second[cut:], "head", 1)], axis=0
        )
        return [own, first, second, third]
    blocks = [own]
    bit = 1
    while bit < size:
        blocks = blocks + [swap(block, "head", bit) for block in blocks]
        bit *= 2
    return blocks


def gather_near(own, *beside):
    return gather_end(own, tuple(after(block, *beside) for block in gather_begin(own)))


def scatter_near(compute, groups):
    size = lax.axis_size("head")
    if size == 4:
        parts = dict(zip(groups[0], compute(groups[0], ())))
        cut = parts[3].shape[0] // 2
        via_first = swap(parts[3][:cut], "head", 1)
        via_second = swap(parts[3][cut:], "head", 2)
        parts.update(zip(groups[1], compute(groups[1], (parts[3],))))
        second = jnp.concatenate([parts[2][:cut] + via_first, parts[2][cut:]], axis=0)
        first = jnp.concatenate([parts[1][:cut], parts[1][cut:] + via_second], axis=0)
        if len(groups) > 2:
            parts.update(zip(groups[2], compute(groups[2], (first, second))))
        return (
            parts[0].astype(jnp.float32)
            + swap(first, "head", 1).astype(jnp.float32)
            + swap(second, "head", 2).astype(jnp.float32)
        ), (first, second)
    parts = compute(list(range(size)), ())
    begun = tuple(parts)
    bit = size // 2
    while bit:
        parts = [parts[k] + swap(parts[k + bit], "head", bit) for k in range(bit)]
        bit //= 2
    return parts[0].astype(jnp.float32), begun


def spread(pieces):
    return [pieces[0]] + [swap(pieces[k], "head", k) for k in range(1, len(pieces))]


def attend_kernel(
    spots, latent, up_weight, cosine, sine, keys, values, out_weight, query, mixed, partial, total
):
    block, head = pl.program_id(0), pl.program_id(1)
    count = spots.shape[0] - 2
    rows, width = query.shape
    place = spots[block]
    raw = dot(latent[...], up_weight[...])
    query[...] = rotate(raw, cosine[...], sine[...]).astype(low)
    row = place * rows + lax.broadcasted_iota(jnp.int32, (rows, 1), 0)
    first, second = spots[count], spots[count + 1]
    begin = jnp.where(row >= second, second, jnp.where(row >= first, first, 0))

    def with_keys(size):
        column = lax.broadcasted_iota(jnp.int32, (rows, size), 1)
        scores = dot(query[...], keys[:size], (1, 1)) * (1.0 / math.sqrt(width))
        scores = jnp.where((column <= row) & (column >= begin), scores, masked_value)
        raised = jnp.exp(scores - jnp.max(scores, axis=1, keepdims=True))
        shares = raised * (1.0 / jnp.sum(raised, axis=1, keepdims=True))
        mixed[...] = dot(shares.astype(low), values[:size]).astype(low)

    for number in range(keys.shape[0] // rows):
        pl.when(place == number)(functools.partial(with_keys, (number + 1) * rows))

    product = dot(mixed[...], out_weight[...])

    @pl.when(head == 0)
    def _():
        total[...] = product

    @pl.when(head > 0)
    def _():
        total[...] += product

    @pl.when(head == pl.num_programs(1) - 1)
    def _():
        partial[...] = total[...].astype(low)


def attend(spots, latent, query_up, cosine, sine, keys, values, out_weight):
    total, rank = latent.shape
    spare, head_width = keys.shape
    blocks = spots.shape[0] - 2
    rows = total // blocks
    heads = query_up.shape[1] // head_width
    width = out_weight.shape[1]
    whole = pl.BlockSpec(keys.shape, lambda i, h, s: (0, 0))
    table = pl.BlockSpec((rows, head_width // 2), lambda i, h, s: (i, 0))
    tile = pl.BlockSpec((rows, head_width), lambda i, h, s: (i, h))
    return pl.pallas_call(
        attend_kernel,
        grid_spec=pltpu.PrefetchScalarGridSpec(
            num_scalar_prefetch=1,
            grid=(blocks, heads),
            in_specs=[
                pl.BlockSpec((rows, rank), lambda i, h, s: (i, 0)),
                pl.BlockSpec((rank, head_width), lambda i, h, s: (0, h)),
                table,
                table,
                whole,
                whole,
                pl.BlockSpec((head_width, width), lambda i, h, s: (h, 0)),
            ],
            out_specs=[tile, tile, pl.BlockSpec((rows, width), lambda i, h, s: (i, 0))],
            scratch_shapes=[pltpu.VMEM((rows, width), jnp.float32)],
        ),
        out_shape=[
            jax.ShapeDtypeStruct((total, heads * head_width), low),
            jax.ShapeDtypeStruct((total, heads * head_width), low),
            jax.ShapeDtypeStruct((total, width), low),
        ],
        compiler_params=pltpu.CompilerParams(vmem_limit_bytes=40 << 20),
        cost_estimate=pl.CostEstimate(
            flops=2 * total * heads * head_width * (rank + width + 5 * spare // 4),
            bytes_accessed=2 * total * (rank + width) + blocks * 2 * query_up.size * 3,
            transcendentals=total * heads * spare,
        ),
    )(spots, latent, query_up, cosine, sine, keys, values, out_weight)


def attend_back_kernel(
    spots,
    branch,
    out_weight,
    query,
    keys,
    values,
    up_weight,
    cosine,
    sine,
    key_before,
    value_before,
    query_back,
    partial,
    key_back,
    value_back,
    total,
    grad_query,
):
    block, head = pl.program_id(0), pl.program_id(1)
    count = spots.shape[0] - 2
    rows, width = query.shape
    place = spots[block]
    scale = 1.0 / math.sqrt(width)
    mixed_back = dot(branch[...], out_weight[...], (1, 1)).astype(low)
    column = place * rows + lax.broadcasted_iota(jnp.int32, (1, rows), 1)
    first, second = spots[count], spots[count + 1]
    begin = jnp.where(column >= second, second, jnp.where(column >= first, first, 0))

    @pl.when((block == 0) & (head == 0))
    def _():
        key_back[...] = key_before[...]
        value_back[...] = value_before[...]

    def with_keys(size):
        row = lax.broadcasted_iota(jnp.int32, (size, rows), 0)
        scores = dot(keys[:size], query[...], (1, 1)) * scale
        scores = jnp.where((row <= column) & (row >= begin), scores, masked_value)
        raised = jnp.exp(scores - jnp.max(scores, axis=0, keepdims=True))
        shares = raised * (1.0 / jnp.sum(raised, axis=0, keepdims=True))
        value_back[:size] += dot(shares.astype(low), mixed_back)
        back = dot(values[:size], mixed_back, (1, 1))
        centre = jnp.sum(shares * back, axis=0, keepdims=True)
        scores_back = (shares * (back - centre)).astype(low)
        key_back[:size] += dot(scores_back, query[...]) * scale
        grad_query[...] = dot(scores_back, keys[:size], (0, 0)) * scale

    for number in range(keys.shape[0] // rows):
        pl.when(place == number)(functools.partial(with_keys, (number + 1) * rows))

    turned = rotate(grad_query[...], cosine[...], -sine[...]).astype(low)
    query_back[...] = turned
    product = dot(turned, up_weight[...], (1, 1))

    @pl.when(head == 0)
    def _():
        total[...] = product

    @pl.when(head > 0)
    def _():
        total[...] += product

    @pl.when(head == pl.num_programs(1) - 1)
    def _():
        partial[...] = total[...].astype(low)


def attend_back(
    spots,
    branch,
    out_weight,
    query,
    keys,
    values,
    query_up,
    cosine,
    sine,
    key_before,
    value_before,
):
    total, width = branch.shape
    spare, head_width = keys.shape
    rank = query_up.shape[0]
    blocks = spots.shape[0] - 2
    rows = total // blocks
    heads = query_up.shape[1] // head_width
    whole = pl.BlockSpec(keys.shape, lambda i, h, s: (0, 0))
    table = pl.BlockSpec((rows, head_width // 2), lambda i, h, s: (i, 0))
    tile = pl.BlockSpec((rows, head_width), lambda i, h, s: (i, h))
    return pl.pallas_call(
        attend_back_kernel,
        grid_spec=pltpu.PrefetchScalarGridSpec(
            num_scalar_prefetch=1,
            grid=(blocks, heads),
            in_specs=[
                pl.BlockSpec((rows, width), lambda i, h, s: (i, 0)),
                pl.BlockSpec((head_width, width), lambda i, h, s: (h, 0)),
                tile,
                whole,
                whole,
                pl.BlockSpec((rank, head_width), lambda i, h, s: (0, h)),
                table,
                table,
                whole,
                whole,
            ],
            out_specs=[
                tile,
                pl.BlockSpec((rows, rank), lambda i, h, s: (i, 0)),
                whole,
                whole,
            ],
            scratch_shapes=[
                pltpu.VMEM((rows, rank), jnp.float32),
                pltpu.VMEM((rows, head_width), jnp.float32),
            ],
        ),
        out_shape=[
            jax.ShapeDtypeStruct((total, heads * head_width), low),
            jax.ShapeDtypeStruct((total, rank), low),
            jax.ShapeDtypeStruct(keys.shape, jnp.float32),
            jax.ShapeDtypeStruct(keys.shape, jnp.float32),
        ],
        compiler_params=pltpu.CompilerParams(vmem_limit_bytes=40 << 20),
        cost_estimate=pl.CostEstimate(
            flops=2 * total * heads * head_width * (rank + width + 25 * spare // 8),
            bytes_accessed=2 * total * (rank + width) + blocks * 2 * query_up.size * 3,
            transcendentals=total * heads * spare,
        ),
    )(
        spots,
        branch,
        out_weight,
        query,
        keys,
        values,
        query_up,
        cosine,
        sine,
        key_before,
        value_before,
    )


def feed_kernel(order, inner, weights, *refs):
    hidden, by_up, by_gate = refs[-3:]
    gate = dot(inner[...], weights[0])
    sigma = 1.0 / (1.0 + jnp.exp(-gate))
    swish = gate * sigma
    up = dot(inner[...], weights[1])
    hidden[...] = (swish * up).astype(low)
    by_gate[...] = swish.astype(low)
    by_up[...] = (up * (sigma * (1.0 + gate * (1.0 - sigma)))).astype(low)


def feed(inner, weights, group, count, earlier):
    rows = inner.shape[0] // len(group)
    width = inner.shape[1]
    part = weights.shape[2]
    shape = jax.ShapeDtypeStruct((rows * count, part), low)
    return pl.pallas_call(
        feed_kernel,
        grid_spec=pltpu.PrefetchScalarGridSpec(
            num_scalar_prefetch=1,
            grid=(len(group),),
            in_specs=[
                pl.BlockSpec((rows, width), lambda i, order: (i, 0)),
                pl.BlockSpec(
                    weights.shape, lambda i, order: (0, 0, 0), pipeline_mode=pl.Buffered(1)
                ),
            ]
            + [pl.BlockSpec(memory_space=pl.ANY)] * len(earlier),
            out_specs=[pl.BlockSpec((rows, part), lambda i, order: (order[i], 0))] * 3,
        ),
        out_shape=[shape, shape, shape],
        input_output_aliases={3 + i: i for i in range(len(earlier))},
        compiler_params=pltpu.CompilerParams(vmem_limit_bytes=40 << 20),
        cost_estimate=pl.CostEstimate(
            flops=4 * inner.size * part,
            bytes_accessed=2 * rows * len(group) * (width + 3 * part) + 2 * weights.size,
            transcendentals=rows * len(group) * part,
        ),
    )(jnp.array(group, jnp.int32), inner, weights, *earlier)


def feed_back_kernel(order, cotangent, down, weights, by_up, by_gate, *refs):
    grads, partial = refs[-2:]
    back = dot(cotangent[...], down[...])
    grad_gate = (back * by_up[...].astype(jnp.float32)).astype(low)
    grad_up = (back * by_gate[...].astype(jnp.float32)).astype(low)
    grads[0] = grad_gate
    grads[1] = grad_up
    partial[...] = (
        dot(grad_gate, weights[0], (1, 1)) + dot(grad_up, weights[1], (1, 1))
    ).astype(low)


def feed_back(cotangent, down, weights, by_up, by_gate, group, count, earlier):
    total, width = cotangent.shape
    rows = total // count
    part = weights.shape[2]
    tile = pl.BlockSpec((rows, part), lambda i, order: (order[i], 0))
    return pl.pallas_call(
        feed_back_kernel,
        grid_spec=pltpu.PrefetchScalarGridSpec(
            num_scalar_prefetch=1,
            grid=(len(group),),
            in_specs=[
                pl.BlockSpec((rows, width), lambda i, order: (order[i], 0)),
                pl.BlockSpec(down.shape, lambda i, order: (0, 0), pipeline_mode=pl.Buffered(1)),
                pl.BlockSpec(
                    weights.shape, lambda i, order: (0, 0, 0), pipeline_mode=pl.Buffered(1)
                ),
                tile,
                tile,
            ]
            + [pl.BlockSpec(memory_space=pl.ANY)] * len(earlier),
            out_specs=[
                pl.BlockSpec((2, rows, part), lambda i, order: (0, order[i], 0)),
                pl.BlockSpec((rows, width), lambda i, order: (i, 0)),
            ],
        ),
        out_shape=[
            jax.ShapeDtypeStruct((2, total, part), low),
            jax.ShapeDtypeStruct((rows * len(group), width), low),
        ],
        input_output_aliases={6 + i: i for i in range(len(earlier))},
        compiler_params=pltpu.CompilerParams(vmem_limit_bytes=48 << 20),
        cost_estimate=pl.CostEstimate(
            flops=6 * rows * len(group) * width * part,
            bytes_accessed=4 * rows * len(group) * (width + 2 * part) + 6 * down.size,
            transcendentals=0,
        ),
    )(jnp.array(group, jnp.int32), cotangent, down, weights, by_up, by_gate, *earlier)


def weight_kernel(left, right, out):
    out[0] = dot(left[...], right[0], (0, 0)).astype(low)


def weight_terms(left, right):
    total, width = left.shape
    number, spare, part = right.shape
    strip = width // lax.axis_size("batch")
    return pl.pallas_call(
        weight_kernel,
        grid=(number, width // strip),
        in_specs=[
            pl.BlockSpec((total, strip), lambda g, i: (0, i)),
            pl.BlockSpec((1, total, part), lambda g, i: (g, 0, 0)),
        ],
        out_specs=pl.BlockSpec((1, strip, part), lambda g, i: (g, i, 0)),
        out_shape=jax.ShapeDtypeStruct((number, width, part), low),
        compiler_params=pltpu.CompilerParams(vmem_limit_bytes=40 << 20),
        cost_estimate=pl.CostEstimate(
            flops=2 * number * total * width * part,
            bytes_accessed=2 * total * (width + number * part) + 2 * number * width * part,
            transcendentals=0,
        ),
    )(left, right)


def sum_over_batch_rows(values):
    return lax.psum_scatter(values, "batch", scatter_dimension=1, tiled=True)


def columns_of(weights, feed_part):
    count = lax.axis_size("head")
    me = lax.axis_index("head")
    depth, strip = weights.shape[:2]
    arrived = spread(
        [
            lax.dynamic_slice_in_dim(weights, (me ^ k) * feed_part, feed_part, 2)
            for k in range(count)
        ]
    )
    columns = jnp.zeros((depth, strip * count, feed_part), low)
    for k in range(count):
        columns = lax.dynamic_update_slice(columns, arrived[k], (0, (me ^ k) * strip, 0))
    return columns


def spread_columns(sums, strip):
    count = lax.axis_size("head")
    me = lax.axis_index("head")
    return spread(
        [lax.dynamic_slice_in_dim(sums, (me ^ k) * strip, strip, 1) for k in range(count)]
    )


def placed_columns(arrived, number):
    me = lax.axis_index("head")
    strip, part = arrived[0].shape[1:]
    gradient = jnp.zeros((strip, part * len(arrived)), jnp.float32)
    for k, block in enumerate(arrived):
        gradient = lax.dynamic_update_slice(
            gradient, block[number].astype(jnp.float32), (0, (me ^ k) * part)
        )
    return gradient


def sum_over_batch(values):
    size = lax.axis_size("batch") // 2
    place = lax.axis_index("batch")
    core, line = place & 1, place >> 1
    half = values.shape[0] // 2
    piece = half // size
    given = swap(lax.dynamic_slice_in_dim(values, (1 - core) * half, half), "batch", 1)
    kept = lax.dynamic_slice_in_dim(values, core * half, half) + given
    pieces = [
        lax.dynamic_slice_in_dim(kept, (line ^ k) * piece, piece) for k in range(size)
    ]
    total = pieces[0].astype(jnp.float32)
    for k in range(1, size):
        total = total + swap(pieces[k], "batch", 2 * k).astype(jnp.float32)
    total = total.astype(values.dtype)
    whole = jnp.zeros((half,) + values.shape[1:], values.dtype)
    for k in range(size):
        block = swap(total, "batch", 2 * k) if k else total
        whole = lax.dynamic_update_slice(whole, block, ((line ^ k) * piece, 0))
    return whole


def sum_over_all(values):
    for axis in ("head", "batch"):
        bit = 1
        while bit < lax.axis_size(axis):
            values = values + swap(values, axis, bit)
            bit *= 2
    return values


def widen_kernel(order, block, *outs):
    begin = 0
    for out in outs:
        out[...] = block[:, begin : begin + out.shape[1]].astype(out.dtype)
        begin += out.shape[1]


def widen(order, blocks, widths):
    count = order.shape[0]
    rows = blocks.shape[0] // count
    return pl.pallas_call(
        widen_kernel,
        grid_spec=pltpu.PrefetchScalarGridSpec(
            num_scalar_prefetch=1,
            grid=(count,),
            in_specs=[pl.BlockSpec((rows, blocks.shape[1]), lambda i, order: (order[i], 0))],
            out_specs=[pl.BlockSpec((rows, width), lambda i, order: (i, 0)) for width in widths],
        ),
        out_shape=[
            jax.ShapeDtypeStruct((blocks.shape[0], width), jnp.float32) for width in widths
        ],
        compiler_params=pltpu.CompilerParams(vmem_limit_bytes=24 << 20),
    )(order, blocks)


def shards(
    tokens,
    attention_gain,
    query_down,
    query_gain,
    query_up,
    key_weight,
    value_weight,
    out_weight,
    feed_gain,
    gate_weight,
    up_weight,
    down_weight,
    lengths,
    cotangent,
):
    rows, width = tokens.shape
    count = lax.axis_size("head")
    me = lax.axis_index("head")
    total = rows * count
    head_width = key_weight.shape[1]
    rank = query_up.shape[0]
    feed_part = gate_weight.shape[1] // count
    strip = gate_weight.shape[0]

    bounds = jnp.cumsum(lengths.reshape(-1), dtype=jnp.int32)
    index = jnp.concatenate(
        [(me ^ k) * rows + jnp.arange(rows, dtype=jnp.int32) for k in range(count)]
    )
    segment = (index >= bounds[0]).astype(jnp.int32) + (index >= bounds[1]).astype(jnp.int32)
    begin = jnp.where(segment == 0, 0, jnp.where(segment == 1, bounds[0], bounds[1]))
    half = head_width // 2
    rates = 10000.0 ** (-2.0 * jnp.arange(half, dtype=jnp.float32) / head_width)
    turns = (index - begin).astype(jnp.float32)[:, None] * rates[None, :]
    cosine, sine = jnp.cos(turns), jnp.sin(turns)
    own_cosine, own_sine = cosine[:rows], sine[:rows]
    ends = bounds[:2]

    def spots(group):
        return jnp.concatenate([me ^ jnp.array(group, jnp.int32), ends])

    def part(values, group):
        return values[group[0] * rows : (group[-1] + 1) * rows]

    groups = sending_order(count)

    def split(values, group):
        return [values[i * rows : (i + 1) * rows] for i in range(len(group))]


    inputs = tokens.astype(jnp.float32)
    normed, first_factor = rescale(inputs, attention_gain)
    normed_low = normed.astype(low)
    latent = dot(normed_low, query_down)
    latent_in, latent_factor = rescale(latent, query_gain)
    key_own = rotate(dot(normed_low, key_weight), own_cosine, own_sine).astype(low)
    value_own = dot(normed_low, value_weight).astype(low)
    lkv_own = jnp.concatenate([latent_in.astype(low), key_own, value_own], axis=1)
    gate_up_columns = columns_of(jnp.stack([gate_weight, up_weight]), feed_part)
    gate_up_columns = after(gate_up_columns, lkv_own)
    gate_up_whole = lax.all_gather(gate_up_columns, "batch", axis=1, tiled=True)
    lkv_blocks = gather_near(lkv_own, gate_up_columns)
    latent_last = lkv_blocks[-1]
    down_columns = columns_of(after(down_weight, latent_last).T[None], feed_part)
    latent_all = jnp.concatenate([block[:, :rank] for block in lkv_blocks], axis=0)
    keys_all, values_all = jnp.zeros((2, total, head_width), low)
    for k in range(count):
        keys_all = lax.dynamic_update_slice(
            keys_all, lkv_blocks[k][:, rank : rank + head_width], ((me ^ k) * rows, 0)
        )
        values_all = lax.dynamic_update_slice(
            values_all, lkv_blocks[k][:, rank + head_width :], ((me ^ k) * rows, 0)
        )
    queries, mixes = {}, {}
    cotangent_begun = gather_begin(after(cotangent, latent_last))

    def attention(group, tie):
        if group == [0]:
            tie += cotangent_begun
        queries[group[0]], mixes[group[0]], partial = attend(
            spots(group),
            after(part(latent_all, group), *tie),
            query_up,
            part(cosine, group),
            part(sine, group),
            keys_all,
            values_all,
            out_weight,
        )
        return split(partial, group)

    attention_part, _ = scatter_near(attention, groups)
    mixed_low = jnp.concatenate([mixes[group[0]] for group in sorted(groups)], axis=0)
    middle = inputs + attention_part
    inner, second_factor = rescale(middle, feed_gain)
    inner_low = inner.astype(low)
    down_whole = lax.all_gather(after(down_columns[0], inner_low), "batch", axis=0, tiled=True)
    found = []

    def forward(blocks, group, *tie):
        rows_in = after(jnp.concatenate(blocks, axis=0), *tie)
        found[:] = feed(rows_in, gate_up_whole, group, count, list(found))

    if count == 4:
        begun = gather_begin(inner_low)
        forward([inner_low], [0])
        begun = tuple(after(block, found[0]) for block in begun)
        inner_blocks = gather_end(inner_low, begun)
        forward(inner_blocks[1:3], [1, 2])
        forward(inner_blocks[3:], [3])
        cotangent_begun = tuple(after(block, *begun) for block in cotangent_begun)
    else:
        inner_blocks = gather_near(inner_low)
        forward(inner_blocks, list(range(count)))
    cotangent_all = jnp.concatenate(gather_end(cotangent, cotangent_begun), axis=0)
    hidden_low, by_up, by_gate = found
    inner_all = jnp.concatenate(inner_blocks, axis=0)
    down_terms = weight_terms(cotangent_all, hidden_low[None])
    down_terms, by_up = lax.optimization_barrier((down_terms, by_up))
    down_sum = sum_over_batch_rows(down_terms)[0]
    found = []
    slice_width = width // count
    normed_later = after(normed_low, down_terms)
    normed_slices = spread(
        [
            lax.dynamic_slice_in_dim(normed_later, (me ^ k) * slice_width, slice_width, 1)
            for k in range(count)
        ]
    )

    def back(group, tie):
        if tie:
            tie += tuple(normed_slices)
        grads, partial = feed_back(
            cotangent_all,
            after(down_whole, *tie),
            gate_up_whole,
            by_up,
            by_gate,
            group,
            count,
            list(found),
        )
        found[:] = [grads]
        return split(partial, group)

    grad_inner, begun = scatter_near(
        back, [groups[0], sum(groups[1:], [])] if len(groups) > 1 else groups
    )
    feed_terms = weight_terms(inner_all, after(found[0], *begun))
    grad_inner, feed_terms, down_sum = lax.optimization_barrier(
        (grad_inner, feed_terms, down_sum)
    )
    feed_sum = sum_over_batch_rows(feed_terms)

    middle_part, feed_gain_part = rescale_back(middle, second_factor, feed_gain, grad_inner)
    grad_middle = cotangent.astype(jnp.float32) + middle_part
    branch_low = grad_middle.astype(low)
    feed_partial = dot(after(hidden_low, branch_low), down_whole, (1, 1)).astype(low)
    branch_all = jnp.concatenate(gather_near(branch_low, feed_partial), axis=0)
    branch_all, feed_partial, down_sum = lax.optimization_barrier(
        (branch_all, feed_partial, down_sum)
    )
    arrived_first = spread_columns(down_sum[None], strip)
    key_grads, value_grads = jnp.zeros((2, total, head_width), jnp.float32)
    query_grads = {}
    totals = [key_grads, value_grads]

    def attention_back(group, tie):
        query_grads[group[0]], partial, totals[0], totals[1] = attend_back(
            spots(group),
            after(part(branch_all, group), *tie),
            out_weight,
            queries[group[0]],
            keys_all,
            values_all,
            query_up,
            part(cosine, group),
            part(sine, group),
            *totals,
        )
        return split(partial, group)

    latent_back, _ = scatter_near(attention_back, groups)
    key_grads, value_grads = totals
    query_grad_low = jnp.concatenate([query_grads[group[0]] for group in sorted(groups)], axis=0)
    key_value_partials = [
        jnp.concatenate(
            [
                lax.dynamic_slice_in_dim(key_grads, (me ^ k) * rows, rows),
                lax.dynamic_slice_in_dim(value_grads, (me ^ k) * rows, rows),
            ],
            axis=1,
        ).astype(low)
        for k in range(count)
    ]
    out_part = dot(mixed_low, branch_all, (0, 0)).astype(low)
    query_part = dot(latent_all, query_grad_low, (0, 0)).astype(low)
    query_part, out_part, arrived_first, feed_sum = lax.optimization_barrier(
        (query_part, out_part, arrived_first, feed_sum)
    )
    key_value_partials = after(key_value_partials, feed_sum)
    key_value_back, _ = scatter_near(
        lambda group, tie: [key_value_partials[k] for k in group], groups
    )
    query_up_gradient, out_gradient = lax.psum((query_part, out_part), "batch")
    latent_grad, query_gain_part = rescale_back(latent, latent_factor, query_gain, latent_back)
    key_back = rotate_back(key_value_back[:, :head_width], own_cosine, own_sine)
    lkv_grad_low = jnp.concatenate(
        [latent_grad, key_back, key_value_back[:, head_width:]], axis=1
    ).astype(low)

    lkv_grad_all = jnp.concatenate(gather_near(lkv_grad_low), axis=0)
    shared_part = dot(jnp.concatenate(normed_slices, axis=0), lkv_grad_all, (0, 0)).astype(low)
    feed_partial = after(feed_partial, shared_part)
    feed_out, _ = scatter_near(
        lambda group, tie: split(part(feed_partial, group), group), groups
    )
    output = (middle + feed_out).astype(low)

    grad_normed = (
        dot(lkv_grad_low[:, :rank], query_down, (1, 1))
        + dot(lkv_grad_low[:, rank : rank + head_width], key_weight, (1, 1))
        + dot(lkv_grad_low[:, rank + head_width :], value_weight, (1, 1))
    )
    input_part, attention_gain_part = rescale_back(
        inputs, first_factor, attention_gain, grad_normed
    )
    input_gradient = grad_middle + input_part
    gains = sum_over_all(
        after(
            jnp.concatenate([attention_gain_part, feed_gain_part, query_gain_part]), shared_part
        ).reshape(-1, 128)
    ).reshape(-1)
    arrived_second = spread_columns(after(feed_sum, shared_part), strip)
    shared_half = sum_over_batch(shared_part)
    blocks = gather_near(shared_half)
    blocks, query_up_gradient, out_gradient = lax.optimization_barrier(
        (blocks, query_up_gradient, out_gradient)
    )
    mine = jnp.concatenate(blocks + [swap(block, "batch", 1) for block in blocks], axis=0)
    spot = jnp.arange(2 * count, dtype=jnp.int32)
    order = ((spot >> 1) ^ me) + count * ((spot & 1) ^ (lax.axis_index("batch") & 1))
    query_down_gradient, key_gradient, value_gradient = widen(
        order, mine, (rank, head_width, head_width)
    )
    return (
        output,
        input_gradient,
        gains[:width],
        query_down_gradient,
        gains[2 * width :],
        query_up_gradient.astype(jnp.float32),
        key_gradient,
        value_gradient,
        out_gradient.astype(jnp.float32),
        gains[width : 2 * width],
        placed_columns(arrived_second, 0),
        placed_columns(arrived_second, 1),
        placed_columns(arrived_first, 0).T,
    )


def solution(mesh):
    rows = P(("batch", "head"), None)
    columns = P(None, ("batch", "head"))
    return jax.shard_map(
        shards,
        mesh=mesh,
        in_specs=(
            rows,
            P(),
            P(),
            P(),
            P(None, "head"),
            P(),
            P(),
            P("head", None),
            P(),
            rows,
            rows,
            columns,
            P("batch", None),
            rows,
        ),
        out_specs=(
            rows,
            rows,
            P(),
            P(),
            P(),
            P(None, "head"),
            P(),
            P(),
            P("head", None),
            P(),
            rows,
            rows,
            columns,
        ),
        check_vma=False,
    )
```
